256 devices in a mesh: row: 16 (over z_hi, x, core), col: 16 (over z_lo, y).
Axes of the slice: x: 4, y: 4, z: 8 (z_hi: 2, z_lo: 4; z = z_hi * 4 + z_lo), core: 2. Of those that a mesh axis runs over, the one named last changes fastest.
Arguments:
- tokens: bfloat16 [131072, 1024], P(('row', 'col')), may hold values from -6 to 6
- gate: bfloat16 [131072, 1024], P('row', 'col'), may hold values from -6 to 6
- filter_spectrum: float32 [2, 256, 128, 1024], P(None, None, None, ('col', 'row')), may hold values from -12 to 12
- skip_gain: float32 [1024], P(('col', 'row')), may hold values from 0.3 to 3
- kept_blocks: int32 [256], replicated, may hold values from 0 to 1023, as said below
- out_weight: bfloat16 [1024, 2048], P('col'), may hold values from -0.1875 to 0.1875
Outputs:
- mixed: bfloat16 [131072, 2048], P(('row', 'col'))
The draws below stay inside these ranges and needn't reach their ends.
Inputs may be any that keep to these rules, and one draw needn't show every extreme that they name: `kept_blocks`: 256 distinct block numbers in no particular order; blocks 0 and 1023 are always among them.
All inputs are finite; a program needn't handle non-finite values.
Results may differ from the reference program's by a relative error of at most 0.0058.
Values may be sent and summed in bfloat16 or wider, within the bound.
A program may use at most 192 MiB of HBM per device.

```python
import math
import jax
import jax.numpy as jnp
from jax import lax

CHANNELS = 1024
OUT_FEATS = 2048
BLOCK = 128
SEQ = 131072
BLOCKS = 1024
KEPT = 256


def draw_kept_blocks(key, part):
    key = jax.random.fold_in(key, 7)
    middle = jax.random.permutation(key, BLOCKS - 2)[:KEPT - 2].astype(jnp.int32) + 1
    bounds = jnp.array([0, BLOCKS - 1], dtype=jnp.int32)
    merged = jnp.concatenate([bounds, middle])
    shuffle = jax.random.permutation(jax.random.fold_in(key, 1), KEPT)
    return merged[shuffle]


def levels(rng, dims, cuts, smallest, high):
    gain, own = 1.0, jax.random.fold_in(rng, 6)
    for axis_at, parts in cuts:
        draws = jnp.exp(jax.random.uniform(jax.random.fold_in(own, axis_at), (parts,), jnp.float32, smallest / len(cuts), high / len(cuts)))
        gain = gain * jnp.repeat(draws, dims[axis_at] // parts).reshape([-1 if axis == axis_at else 1 for axis in range(len(dims))])
    return gain


def bell_draw(key, shape, scale, bound, pieces=(), kind=jnp.bfloat16):
    result = jax.random.normal(key, shape, jnp.float32) * scale
    if len(pieces) > 0:
        result = levels(key, shape, pieces, -0.22, 0.18) * result
    return jnp.clip(result, min=-bound, max=bound).astype(kind)


def setup_inputs(seed: int = 0) -> dict:
    splits = jax.random.split(jax.random.key(seed), 7)
    tokens = bell_draw(splits[0], (SEQ, CHANNELS), 1.0, 6.0, ((0, 256),))
    gate = bell_draw(splits[1], (SEQ, CHANNELS), 1.0, 6.0, ((0, 16), (1, 16)))
    filter_spectrum = bell_draw(splits[2], (2, KEPT, BLOCK, CHANNELS), 2.0, 12.0, ((3, 256),), jnp.float32)
    skip_gain = jnp.clip(jnp.exp(math.log(3.0) - 2.3025851 * jax.random.uniform(splits[3], (CHANNELS,), jnp.float32) ** levels(splits[3], (CHANNELS,), ((0, 256),), -0.2, 0.2)), 0.3, 3.0)
    kept_blocks = draw_kept_blocks(jax.random.fold_in(splits[6], 71), 0)
    out_weight = bell_draw(splits[5], (CHANNELS, OUT_FEATS), CHANNELS ** -0.5, 0.1875, ((0, 16),))
    return {"tokens": tokens, "gate": gate, "filter_spectrum": filter_spectrum, "skip_gain": skip_gain, "kept_blocks": kept_blocks, "out_weight": out_weight}


def reference(tokens, gate, filter_spectrum, skip_gain, kept_blocks, out_weight):
    widened = tokens.astype(jnp.float32)
    spectrum = jnp.fft.fft(widened, axis=0).reshape(BLOCKS, BLOCK, CHANNELS)
    chosen = spectrum[kept_blocks]
    response = (filter_spectrum[0] + 1j * filter_spectrum[1]) * chosen
    full_response = jnp.zeros_like(spectrum).at[kept_blocks].set(response)
    convolved = jnp.fft.ifft(full_response.reshape(SEQ, CHANNELS), axis=0).real.astype(jnp.float32)
    convolved = (convolved + skip_gain[None, :] * widened).astype(jnp.bfloat16)
    convolved = lax.optimization_barrier(convolved)
    gated = (convolved.astype(jnp.float32) * gate.astype(jnp.float32)).astype(jnp.bfloat16)
    return jnp.dot(gated, out_weight, preferred_element_type=jnp.float32).astype(jnp.bfloat16)
```

```python
import functools

import jax
import jax.numpy as jnp
import numpy as np
from jax import lax
from jax.experimental import pallas as pl
from jax.experimental.pallas import tpu as pltpu
from jax.sharding import PartitionSpec as P

SEQ = 131072
BLOCK = 128
BLOCKS = 1024
KEPT = 256
DEVICES = 256
TOKENS = SEQ // DEVICES
HALF = TOKENS
WIDTH = 4
CHUNKS = 4
TILE = 16
FEATS = 2048
MESH = pl.DeviceIdType.MESH
BF16, F32 = jnp.bfloat16, jnp.float32


def split(table):
    high = table.astype(BF16)
    low = (table - high.astype(np.float64)).astype(BF16)
    return np.stack([high, low])


def tables():
    grid = np.arange(BLOCKS)
    angle = 2.0 * np.pi * (np.outer(grid, grid) % BLOCKS) / BLOCKS
    blocks = np.concatenate([split(np.cos(angle)), split(np.sin(angle))])
    offsets = np.arange(BLOCK)
    angle = 2.0 * np.pi * np.outer(offsets, grid) / SEQ
    twist = np.stack([np.cos(angle), np.sin(angle)]).astype(np.float32)
    angle = 2.0 * np.pi * (np.outer(offsets, offsets) % BLOCK) / BLOCK
    cos, sin = np.cos(angle), np.sin(angle)
    first = np.zeros((2, 2, BLOCK, BLOCK, 2))
    last = np.zeros((BLOCK, 2, 2, 2, BLOCK))
    for p in range(2):
        first[p, 0, :, :, p], first[p, 1, :, :, p] = cos, -sin
        last[:, p, p, 0, :], last[:, p, p, 1, :] = cos, -sin
    first = split(first.reshape(512, 256))
    last = split(last.reshape(256, 512))
    pack = np.zeros((32, WIDTH, CHUNKS, CHUNKS, 32, WIDTH), np.float32)
    for o in range(32):
        for c in range(WIDTH):
            for h in range(CHUNKS):
                pack[o, c, h, h, o, c] = 1.0
    pack = pack.reshape(512, 512).astype(BF16)
    rows = np.arange(256).reshape(16, WIDTH, CHUNKS)
    eye = np.eye(256, dtype=np.float32)
    fold = eye[rows.transpose(1, 2, 0).reshape(-1)]
    order = eye[rows.transpose(2, 0, 1).reshape(-1)]
    moves = np.stack([fold, fold.T, order]).astype(BF16)
    return blocks, twist, first, last, pack, moves


def dot(a, b):
    return lax.dot_general(a, b, (((1,), (0,)), ((), ())), preferred_element_type=F32)


def dot_nt(a, b):
    return lax.dot_general(a, b, (((1,), (1,)), ((), ())), preferred_element_type=F32)


def dot_tn(a, b):
    return lax.dot_general(a, b, (((0,), (0,)), ((), ())), preferred_element_type=F32)


def halves(value):
    high = value.astype(BF16)
    return high, (value - high.astype(F32)).astype(BF16)


def kept_table(kept, blocks):
    row = lax.broadcasted_iota(jnp.int32, (KEPT, KEPT), 0)
    lane = lax.broadcasted_iota(jnp.int32, (KEPT, KEPT), 1)
    column = jnp.sum(jnp.where(row == lane, kept.astype(F32), 0.0), axis=1, keepdims=True)
    lane = lax.broadcasted_iota(jnp.int32, (KEPT, BLOCKS), 1).astype(F32)
    pick = jnp.where(lane == column, 1.0, 0.0).astype(BF16)
    return [dot(pick, blocks(i)).astype(BF16) for i in range(4)]


def kernel(
    tokens, gate, filt, skip, kept, weight, blocks, twist, first, last, pack, moves,
    out,
    tok_v, filt_v, blocks_v, twist_v, first_v, last_v, pack_v, moves_v,
    sent, got, z, tab, turn, resp, back, conv, packed, returned, gate_v, gated, w_v,
    local, own, a_send, a_recv, g_send, g_recv, w_send, w_recv, b_send, b_recv,
):
    row, col = lax.axis_index("row"), lax.axis_index("col")
    zh, x, core = row // 8, lax.rem(row, 8) // 2, lax.rem(row, 2)
    zl, y = col // 4, lax.rem(col, 4)
    as_tokens, as_channels = row * 16 + col, col * 16 + row

    barrier = pltpu.get_barrier_semaphore()

    @pl.loop(1, DEVICES)
    def _(s):
        other = (lax.rem(row + s // 16, 16), lax.rem(col + lax.rem(s, 16), 16))
        pl.semaphore_signal(barrier, inc=1, device_id=other, device_id_type=MESH)

    loads = [
        pltpu.make_async_copy(src, dst, local.at[i])
        for i, (src, dst) in enumerate(
            [(tokens, tok_v), (pack, pack_v), (blocks, blocks_v), (moves, moves_v), (first, first_v),
             (twist, twist_v), (filt, filt_v), (last, last_v)]
        )
    ]
    for load in loads:
        load.start()
    slice_at = pl.ds(pl.multiple_of((core * 4 + x) * 256, 256), 256)
    own_weight = pltpu.make_async_copy(weight.at[:, slice_at], w_v.at[zl, y, :, slice_at], own.at[0])
    own_weight.start()

    loads[0].wait()
    loads[1].wait()

    @pl.loop(0, 8)
    def _(g):
        at = pl.ds(pl.multiple_of(g * 128, 128), 128)
        wide = jnp.concatenate([tok_v[pl.ds(h * 128, 128), at] for h in range(CHUNKS)], axis=1)
        sent[pl.ds(pl.multiple_of(g * 512, 512), 512), :] = dot_nt(pack_v[...], wide).astype(BF16)

    pl.semaphore_wait(barrier, DEVICES - 1)

    def tile(index):
        return pl.ds(pl.multiple_of(index * TILE, TILE), TILE)

    def weight_copy(stage, src, dst, device):
        return pltpu.make_async_remote_copy(
            src_ref=src, dst_ref=dst, send_sem=w_send.at[stage], recv_sem=w_recv.at[stage],
            device_id=device, device_id_type=MESH,
        )

    for s in range(1, 4):
        weight_copy(
            0, weight.at[:, slice_at], w_v.at[zl, y, :, slice_at], (row, lax.rem(zl + s, 4) * 4 + y)
        ).start()

    own_tile = pltpu.make_async_copy(sent.at[tile(as_channels)], got.at[tile(as_tokens)], a_recv)
    own_tile.start()

    @pl.loop(1, DEVICES)
    def _(s):
        to_row, to_col = lax.rem(row + s // 16, 16), lax.rem(col + lax.rem(s, 16), 16)
        pltpu.make_async_remote_copy(
            src_ref=sent.at[tile(to_col * 16 + to_row)], dst_ref=got.at[tile(as_tokens)],
            send_sem=a_send, recv_sem=a_recv, device_id=(to_row, to_col), device_id_type=MESH,
        ).start()

    for load in loads[2:]:
        load.wait()
    cos_high, cos_low, sin_high, sin_low = kept_table(kept[...], lambda i: blocks_v[i])
    tab[0, 0:KEPT, :] = cos_high
    tab[0, KEPT:, :] = sin_high
    tab[1, 0:KEPT, :] = cos_low
    tab[1, KEPT:, :] = sin_low

    def weight_wait(sem, stage, ref):
        pltpu.make_async_copy(ref, ref, sem.at[stage]).wait()

    own_weight.wait()
    weight_wait(w_recv, 0, w_v.at[pl.ds(0, 3), 0, :, pl.ds(0, 256)])
    for s in range(1, 4):
        part = w_v.at[:, y, :, slice_at]
        weight_copy(1, part, part, (row, zl * 4 + lax.rem(y + s, 4))).start()

    pltpu.make_async_copy(got, got, a_recv).wait()

    own_gate = pltpu.make_async_copy(
        gate.at[:, pl.ds(pl.multiple_of(col * TOKENS, TOKENS), TOKENS)], gate_v.at[col], g_recv
    )
    own_gate.start()

    @pl.loop(1, 16)
    def _(s):
        to_col = lax.rem(col + s, 16)
        pltpu.make_async_remote_copy(
            src_ref=gate.at[:, pl.ds(pl.multiple_of(to_col * TOKENS, TOKENS), TOKENS)],
            dst_ref=gate_v.at[col], send_sem=g_send, recv_sem=g_recv,
            device_id=(row, to_col), device_id_type=MESH,
        ).start()

    weight_wait(w_recv, 1, w_v.at[:, pl.ds(0, 3), :, pl.ds(0, 256)])
    for s in range(1, 4):
        part = w_v.at[:, :, :, slice_at]
        weight_copy(2, part, part, (zh * 8 + lax.rem(x + s, 4) * 2 + core, col)).start()

    @pl.loop(0, 16)
    def _(g):
        rows = dot(moves_v[0], got[pl.ds(pl.multiple_of(g * 256, 256), 256), :]).astype(BF16)
        for c in range(WIDTH):
            for h in range(CHUNKS):
                z[c, tile(g), pl.ds(h * 128, 128)] = rows[(c * 4 + h) * 16 : (c * 4 + h) * 16 + 16, :]

    @pl.loop(0, WIDTH)
    def _(c):
        signal = z[c]
        spread = dot(first_v[0], signal) + dot(first_v[1], signal)
        for p in range(2):
            at = pl.ds(p * HALF, HALF)
            re, im = spread[p * 256 : p * 256 + 128], spread[p * 256 + 128 : p * 256 + 256]
            cos, sin = twist_v[0, :, at], twist_v[1, :, at]
            turn[0, 0:128, at], turn[1, 0:128, at] = halves(re * cos + im * sin)
            turn[0, 128:256, at], turn[1, 128:256, at] = halves(im * cos - re * sin)
        spec = dot_nt(tab[0], turn[0]) + dot_nt(tab[1], turn[0]) + dot_nt(tab[0], turn[1])
        spec_re = spec[:KEPT, :128] + spec[KEPT:, 128:]
        spec_im = spec[:KEPT, 128:] - spec[KEPT:, :128]
        filt_re, filt_im = filt_v[0, c], filt_v[1, c]
        re = halves(filt_re * spec_re - filt_im * spec_im)
        im = halves(filt_re * spec_im + filt_im * spec_re)
        for i in range(2):
            resp[i, 0:KEPT, 0:128] = re[i]
            resp[i, 0:KEPT, 128:256] = im[i]
            resp[i, KEPT:, 0:128] = -im[i]
            resp[i, KEPT:, 128:256] = re[i]
        wave = dot_tn(resp[0], tab[0]) + dot_tn(resp[1], tab[0]) + dot_tn(resp[0], tab[1])
        for p in range(2):
            at = pl.ds(p * HALF, HALF)
            re, im = wave[:128, p * HALF : p * HALF + HALF], wave[128:, p * HALF : p * HALF + HALF]
            cos, sin = twist_v[0, :, at], twist_v[1, :, at]
            at = p * 256
            back[0, at : at + 128, :], back[1, at : at + 128, :] = halves(re * cos - im * sin)
            back[0, at + 128 : at + 256, :], back[1, at + 128 : at + 256, :] = halves(im * cos + re * sin)
        result = dot(last_v[0], back[0]) + dot(last_v[1], back[0]) + dot(last_v[0], back[1])
        conv[c] = (result * (1.0 / SEQ) + skip[c] * signal.astype(F32)).astype(BF16)

    @pl.loop(0, 16)
    def _(g):
        rows = jnp.concatenate(
            [conv[c, tile(g), pl.ds(h * 128, 128)] for c in range(WIDTH) for h in range(CHUNKS)], axis=0
        )
        packed[pl.ds(pl.multiple_of(g * 256, 256), 256), :] = dot(moves_v[1], rows).astype(BF16)

    own_back = pltpu.make_async_copy(packed.at[tile(as_tokens)], returned.at[tile(as_channels)], b_recv)
    own_back.start()

    @pl.loop(1, DEVICES)
    def _(s):
        to_row, to_col = lax.rem(row + s // 16, 16), lax.rem(col + lax.rem(s, 16), 16)
        pltpu.make_async_remote_copy(
            src_ref=packed.at[tile(to_row * 16 + to_col)], dst_ref=returned.at[tile(as_channels)],
            send_sem=b_send, recv_sem=b_recv, device_id=(to_row, to_col), device_id_type=MESH,
        ).start()

    weight_wait(w_recv, 2, w_v.at[:, :, :, pl.ds(0, 768)])
    half = w_v.at[:, :, :, pl.ds(pl.multiple_of(core * 1024, 1024), 1024)]
    weight_copy(3, half, half, (row + 1 - 2 * core, col)).start()

    pltpu.make_async_copy(gate_v, gate_v, g_recv).wait()
    weight_wait(w_recv, 3, w_v.at[:, :, :, pl.ds(0, 1024)])
    pltpu.make_async_copy(returned, returned, b_recv).wait()

    @pl.loop(0, 16)
    def _(g):
        rows = dot(moves_v[2], returned[pl.ds(pl.multiple_of(g * 256, 256), 256), :])
        for h in range(CHUNKS):
            at = pl.ds(h * 128, 128)
            piece = rows[h * 64 : h * 64 + 64] * gate_v[g, :, at].astype(F32)
            gated[pl.ds(pl.multiple_of(g * 64, 64), 64), at] = piece.astype(BF16)

    @pl.loop(0, 4)
    def _(n):
        at = pl.ds(pl.multiple_of(n * 512, 512), 512)
        out[:, at] = dot_tn(gated[...], w_v[:, :, :, at].reshape(1024, 512)).astype(BF16)

    pltpu.make_async_copy(sent.at[pl.ds(0, 4080)], sent.at[pl.ds(0, 4080)], a_send).wait()
    pltpu.make_async_copy(packed.at[pl.ds(0, 4080)], packed.at[pl.ds(0, 4080)], b_send).wait()
    pltpu.make_async_copy(gate_v.at[pl.ds(0, 15)], gate_v.at[pl.ds(0, 15)], g_send).wait()
    weight_wait(w_send, 0, w_v.at[pl.ds(0, 3), 0, :, pl.ds(0, 256)])
    weight_wait(w_send, 1, w_v.at[:, pl.ds(0, 3), :, pl.ds(0, 256)])
    weight_wait(w_send, 2, w_v.at[:, :, :, pl.ds(0, 768)])
    weight_wait(w_send, 3, w_v.at[:, :, :, pl.ds(0, 1024)])


def on_device(tokens, gate, filter_spectrum, skip_gain, kept_blocks, out_weight):
    blocks, twist, first, last, pack, moves = (jnp.asarray(t) for t in tables())
    filt = jnp.transpose(filter_spectrum, (0, 3, 1, 2))
    hbm = pl.BlockSpec(memory_space=pl.ANY)
    vmem = pl.BlockSpec(memory_space=pltpu.VMEM)
    smem = pl.BlockSpec(memory_space=pltpu.SMEM)
    like = lambda t: pltpu.VMEM(t.shape, t.dtype)
    return pl.pallas_call(
        kernel,
        out_shape=jax.ShapeDtypeStruct((TOKENS, FEATS), BF16),
        in_specs=[hbm, hbm, hbm, smem, vmem, hbm, hbm, hbm, hbm, hbm, hbm, hbm],
        out_specs=vmem,
        scratch_shapes=[
            like(tokens), like(filt), like(blocks), like(twist), like(first), like(last), like(pack), like(moves),
            pltpu.VMEM((4096, 128), BF16),
            pltpu.VMEM((4096, 128), BF16),
            pltpu.VMEM((WIDTH, 256, 512), BF16),
            pltpu.VMEM((2, 2 * KEPT, BLOCKS), BF16),
            pltpu.VMEM((2, 256, BLOCKS), BF16),
            pltpu.VMEM((2, 2 * KEPT, 256), BF16),
            pltpu.VMEM((2, 512, 512), BF16),
            pltpu.VMEM((WIDTH, 256, 512), BF16),
            pltpu.VMEM((4096, 128), BF16),
            pltpu.VMEM((4096, 128), BF16),
            pltpu.VMEM((16, 64, TOKENS), BF16),
            pltpu.VMEM((1024, TOKENS), BF16),
            pltpu.VMEM((4, 4, 64, FEATS), BF16),
            pltpu.SemaphoreType.DMA((8,)),
            pltpu.SemaphoreType.DMA((1,)),
            pltpu.SemaphoreType.DMA,
            pltpu.SemaphoreType.DMA,
            pltpu.SemaphoreType.DMA,
            pltpu.SemaphoreType.DMA,
            pltpu.SemaphoreType.DMA((4,)),
            pltpu.SemaphoreType.DMA((4,)),
            pltpu.SemaphoreType.DMA,
            pltpu.SemaphoreType.DMA,
        ],
        compiler_params=pltpu.CompilerParams(
            collective_id=0, has_side_effects=True, vmem_limit_bytes=56 * 1024 * 1024
        ),
    )(tokens, gate.T, filt, skip_gain, kept_blocks.reshape(1, KEPT), out_weight, blocks, twist, first, last, pack, moves)


def solution(mesh):
    return jax.shard_map(
        on_device,
        mesh=mesh,
        in_specs=(
            P(("row", "col"), None),
            P("row", "col"),
            P(None, None, None, ("col", "row")),
            P(("col", "row")),
            P(),
            P("col", None),
        ),
        out_specs=P(("row", "col"), None),
        check_vma=False,
    )
```

```python
import functools

import jax
import jax.numpy as jnp
import numpy as np
from jax import lax
from jax.experimental import pallas as pl
from jax.experimental.pallas import tpu as pltpu
from jax.sharding import PartitionSpec as P

SEQ = 131072
BLOCK = 128
BLOCKS = 1024
KEPT = 256
DEVICES = 256
TOKENS = SEQ // DEVICES
PAIRS = BLOCK // 2
WIDTH = 4
CHUNKS = 4
TILE = 16
FEATS = 2048
MESH = pl.DeviceIdType.MESH
BF16, F32 = jnp.bfloat16, jnp.float32


def split(table):
    high = table.astype(BF16)
    low = (table - high.astype(np.float64)).astype(BF16)
    return np.stack([high, low])


def tables():
    grid = np.arange(BLOCKS)
    angle = 2.0 * np.pi * (np.outer(2 * grid + 1, grid) % (2 * BLOCKS)) / (2 * BLOCKS)
    blocks = np.concatenate([split(np.cos(angle)), split(np.sin(angle))])
    pairs = np.arange(PAIRS)
    angle = 2.0 * np.pi * np.outer(pairs, grid) / SEQ
    cos, sin = np.cos(angle), np.sin(angle)
    masked = cos.copy()
    masked[0] = 0.0
    twist = np.stack([cos, sin, masked]).astype(np.float32)
    angle = 2.0 * np.pi * PAIRS * grid / SEQ
    edge = np.stack([np.cos(angle), np.sin(angle)]).astype(np.float32)
    j = np.arange(BLOCK)
    sign = (-1.0) ** j
    angle = 2.0 * np.pi * (np.outer(pairs, j) % BLOCK) / BLOCK
    real, imag = sign * np.cos(angle), -sign * np.sin(angle)
    imag[0] = 1.0
    first = np.zeros((2, 2, PAIRS, BLOCK, 2))
    for p in range(2):
        first[p, 0, :, :, p], first[p, 1, :, :, p] = real, imag
    first = first.reshape(256, 256)
    last = split(first.T.copy())
    first = split(first)
    pack = np.zeros((32, WIDTH, CHUNKS, CHUNKS, 32, WIDTH), np.float32)
    for o in range(32):
        for c in range(WIDTH):
            for h in range(CHUNKS):
                pack[o, c, h, h, o, c] = 1.0
    pack = pack.reshape(512, 512).astype(BF16)
    rows = np.arange(256).reshape(16, WIDTH, CHUNKS)
    eye = np.eye(256, dtype=np.float32)
    fold = eye[rows.transpose(1, 2, 0).reshape(-1)]
    rows = rows.reshape(2, 8, WIDTH, CHUNKS)
    order = eye[rows.transpose(0, 3, 1, 2).reshape(-1)]
    moves = np.stack([fold, fold.T, order]).astype(BF16)
    offsets = np.concatenate([64 + pairs, [0], 64 - pairs[1:]])
    mirror = np.eye(BLOCK, dtype=np.float32)[offsets].astype(BF16)
    return blocks, twist, edge, first, last, pack, moves, mirror


def dot(a, b):
    return lax.dot_general(a, b, (((1,), (0,)), ((), ())), preferred_element_type=F32)


def dot_nt(a, b):
    return lax.dot_general(a, b, (((1,), (1,)), ((), ())), preferred_element_type=F32)


def dot_tn(a, b):
    return lax.dot_general(a, b, (((0,), (0,)), ((), ())), preferred_element_type=F32)


def halves(value):
    high = value.astype(BF16)
    return high, (value - high.astype(F32)).astype(BF16)


def kept_table(kept, blocks):
    row = lax.broadcasted_iota(jnp.int32, (KEPT, KEPT), 0)
    lane = lax.broadcasted_iota(jnp.int32, (KEPT, KEPT), 1)
    column = jnp.sum(jnp.where(row == lane, kept.astype(F32), 0.0), axis=1, keepdims=True)
    lane = lax.broadcasted_iota(jnp.int32, (KEPT, BLOCKS), 1).astype(F32)
    pick = jnp.where(lane == column, 1.0, 0.0).astype(BF16)
    return [dot(pick, blocks[i]).astype(BF16) for i in range(4)]


def prepare(kept, blocks_v, filt_v, mirror_v, tab, filt_p):
    cos_high, cos_low, sin_high, sin_low = kept_table(kept[...], blocks_v)
    tab[0, 0:KEPT, :] = cos_high
    tab[0, KEPT:, :] = sin_high
    tab[1, 0:KEPT, :] = cos_low
    tab[1, KEPT:, :] = sin_low
    for i in range(2):
        for c in range(WIDTH):
            high, low = halves(filt_v[i, c])
            filt_p[i, c] = dot_nt(mirror_v[...], high) + dot_nt(mirror_v[...], low)


def convolve(z, first_v, last_v, twist_v, edge_v, tab, filt_p, skip, ends, turn, spec, resp, wave, back, conv):
    @pl.loop(0, WIDTH)
    def _(c):
        signal = z[c]
        spread = dot(first_v[0], signal) + dot(first_v[1], signal)
        rows = pl.ds(pl.multiple_of(c * 128, 128), 128)
        for p in range(2):
            at = pl.ds(p * TOKENS, TOKENS)
            re, im = spread[p * 128 : p * 128 + 64], spread[p * 128 + 64 : p * 128 + 128]
            cos, sin, masked = twist_v[0, :, at], twist_v[1, :, at], twist_v[2, :, at]
            both = jnp.concatenate([re * cos + im * sin, im * masked - re * sin], axis=0)
            turn[0, rows, at], turn[1, rows, at] = halves(both)
            ends[pl.ds(c, 1), at] = im[0:1]

    edge = ends[0:4, :]
    both = [edge * edge_v[0:1, :], edge * -edge_v[1:2, :], jnp.zeros((8, BLOCKS), F32)]
    turn[0, 512:528, :], turn[1, 512:528, :] = halves(jnp.concatenate(both, axis=0))

    spec[...] = dot_nt(turn[0], tab[0]) + dot_nt(turn[1], tab[0]) + dot_nt(turn[0], tab[1])

    top = lax.broadcasted_iota(jnp.int32, (PAIRS, KEPT), 0) == 0
    ends_re, ends_im = [], []
    for c in range(WIDTH):
        at = c * 128
        cos_re, sin_re = spec[at : at + 64, :KEPT], spec[at : at + 64, KEPT:]
        cos_im, sin_im = spec[at + 64 : at + 128, :KEPT], spec[at + 64 : at + 128, KEPT:]
        up_re, up_im = cos_re + sin_im, cos_im - sin_re
        edge_re = spec[512 + c : 513 + c, :KEPT] - spec[516 + c : 517 + c, KEPT:]
        edge_im = -spec[516 + c : 517 + c, :KEPT] - spec[512 + c : 513 + c, KEPT:]
        down_re = jnp.where(top, edge_re, cos_re - sin_im)
        down_im = jnp.where(top, edge_im, -cos_im - sin_re)
        filt_re, filt_im = filt_p[0, c, 0:64], filt_p[1, c, 0:64]
        up_re, up_im = filt_re * up_re - filt_im * up_im, filt_re * up_im + filt_im * up_re
        filt_re, filt_im = filt_p[0, c, 64:128], filt_p[1, c, 64:128]
        down_re, down_im = filt_re * down_re - filt_im * down_im, filt_re * down_im + filt_im * down_re
        ends_re.append(jnp.concatenate([down_re[0:1], -down_im[0:1]], axis=1))
        ends_im.append(jnp.concatenate([-down_im[0:1], -down_re[0:1]], axis=1))
        down_re, down_im = jnp.where(top, 0.0, down_re), jnp.where(top, 0.0, down_im)
        both = jnp.concatenate(
            [
                jnp.concatenate([up_re + down_re, -(up_im + down_im)], axis=1),
                jnp.concatenate([up_im - down_im, up_re - down_re], axis=1),
            ],
            axis=0,
        )
        resp[0, at : at + 128, :], resp[1, at : at + 128, :] = halves(both)
    both = jnp.concatenate(ends_re + ends_im + [jnp.zeros((8, 2 * KEPT), F32)], axis=0)
    resp[0, 512:528, :], resp[1, 512:528, :] = halves(both)

    wave[...] = dot(resp[0], tab[0]) + dot(resp[1], tab[0]) + dot(resp[0], tab[1])
    edge = wave[512:516, :] * edge_v[0:1, :] - wave[516:520, :] * edge_v[1:2, :]
    ends[0:4, :] = edge

    @pl.loop(0, WIDTH)
    def _(c):
        top = lax.broadcasted_iota(jnp.int32, (PAIRS, TOKENS), 0) == 0
        start = pl.multiple_of(c * 128, 128)
        for p in range(2):
            at = pl.ds(p * TOKENS, TOKENS)
            re, im = wave[pl.ds(start, 64), at], wave[pl.ds(start + 64, 64), at]
            cos, sin = twist_v[0, :, at], twist_v[1, :, at]
            low = jnp.where(top, ends[pl.ds(c, 1), at], im * cos + re * sin)
            both = jnp.concatenate([re * cos - im * sin, low], axis=0)
            back[0, p * 128 : p * 128 + 128, :], back[1, p * 128 : p * 128 + 128, :] = halves(both)
        result = dot(last_v[0], back[0]) + dot(last_v[1], back[0]) + dot(last_v[0], back[1])
        conv[c] = (result * (1.0 / SEQ) + skip[c] * z[c].astype(F32)).astype(BF16)


def kernel(
    tokens, gate, filt, skip, kept, weight, blocks, twist, edge, first, last, pack, moves, mirror,
    out,
    tok_v, filt_v, blocks_v, twist_v, edge_v, first_v, last_v, pack_v, moves_v, mirror_v,
    sent, got, z, tab, filt_p, ends, turn, spec, resp, wave, back, conv, packed, returned, near, near_gate, near_out,
    gate_v, gated, w_v,
    local, own, a_send, a_recv, g_send, g_recv, w_send, w_recv, b_send, b_recv, n_send, n_recv, m_send, m_recv,
):
    row, col = lax.axis_index("row"), lax.axis_index("col")
    zh, x, core = row // 8, lax.rem(row, 8) // 2, lax.rem(row, 2)
    low_row = lax.rem(row, 8)
    zl, y = col // 4, lax.rem(col, 4)
    as_tokens, as_channels = row * 16 + col, col * 16 + row

    barrier = pltpu.get_barrier_semaphore()

    @pl.loop(1, DEVICES)
    def _(s):
        other = (lax.rem(row + s // 16, 16), lax.rem(col + lax.rem(s, 16), 16))
        pl.semaphore_signal(barrier, inc=1, device_id=other, device_id_type=MESH)

    same = pl.multiple_of(zh * 32, 32)
    cross = pl.multiple_of(32 - zh * 32, 32)
    loads = [
        pltpu.make_async_copy(src, dst, local.at[i])
        for i, (src, dst) in enumerate(
            [(tokens, tok_v), (pack, pack_v), (blocks, blocks_v), (moves, moves_v), (first, first_v),
             (twist, twist_v), (last, last_v), (edge, edge_v), (mirror, mirror_v),
             (gate.at[pl.ds(same, 32), :], near_gate), (filt, filt_v)]
        )
    ]
    for load in loads:
        load.start()
    slice_at = pl.ds(pl.multiple_of((core * 4 + x) * 256, 256), 256)
    own_weight = pltpu.make_async_copy(weight.at[:, slice_at], w_v.at[zl, y, :, slice_at], own.at[0])
    own_weight.start()

    loads[0].wait()
    loads[1].wait()

    @pl.loop(0, 8)
    def _(g):
        at = pl.ds(pl.multiple_of(g * 128, 128), 128)
        wide = jnp.concatenate([tok_v[pl.ds(h * 128, 128), at] for h in range(CHUNKS)], axis=1)
        sent[pl.ds(pl.multiple_of(g * 512, 512), 512), :] = dot_nt(pack_v[...], wide).astype(BF16)

    pl.semaphore_wait(barrier, DEVICES - 1)

    def tile(index):
        return pl.ds(pl.multiple_of(index * TILE, TILE), TILE)

    def weight_copy(stage, src, dst, device):
        return pltpu.make_async_remote_copy(
            src_ref=src, dst_ref=dst, send_sem=w_send.at[stage], recv_sem=w_recv.at[stage],
            device_id=device, device_id_type=MESH,
        )

    own_tile = pltpu.make_async_copy(sent.at[tile(as_channels)], got.at[tile(as_tokens)], a_recv)
    own_tile.start()

    @pl.loop(1, DEVICES)
    def _(s):
        to_row, to_col = lax.rem(row + s // 16, 16), lax.rem(col + lax.rem(s, 16), 16)
        pltpu.make_async_remote_copy(
            src_ref=sent.at[tile(to_col * 16 + to_row)], dst_ref=got.at[tile(as_tokens)],
            send_sem=a_send, recv_sem=a_recv, device_id=(to_row, to_col), device_id_type=MESH,
        ).start()

    for s in range(1, 4):
        weight_copy(
            0, weight.at[:, slice_at], w_v.at[zl, y, :, slice_at], (row, lax.rem(zl + s, 4) * 4 + y)
        ).start()

    for load in loads[2:]:
        load.wait()
    prepare(kept, blocks_v, filt_v, mirror_v, tab, filt_p)

    def weight_wait(sem, stage, ref):
        pltpu.make_async_copy(ref, ref, sem.at[stage]).wait()

    own_weight.wait()
    weight_wait(w_recv, 0, w_v.at[pl.ds(0, 3), 0, :, pl.ds(0, 256)])
    for s in range(1, 4):
        part = w_v.at[:, y, :, slice_at]
        weight_copy(1, part, part, (row, zl * 4 + lax.rem(y + s, 4))).start()

    pltpu.make_async_copy(got, got, a_recv).wait()

    def gate_at(to_col):
        return gate.at[pl.ds(cross, 32), pl.ds(pl.multiple_of(to_col * TOKENS, TOKENS), TOKENS)]

    own_gate = pltpu.make_async_copy(gate_at(col), gate_v.at[col], g_recv)
    own_gate.start()

    @pl.loop(1, 16)
    def _(s):
        to_col = lax.rem(col + s, 16)
        pltpu.make_async_remote_copy(
            src_ref=gate_at(to_col), dst_ref=gate_v.at[col], send_sem=g_send, recv_sem=g_recv,
            device_id=(row, to_col), device_id_type=MESH,
        ).start()

    weight_wait(w_recv, 1, w_v.at[:, pl.ds(0, 3), :, pl.ds(0, 256)])
    for s in range(1, 4):
        part = w_v.at[:, :, :, slice_at]
        weight_copy(2, part, part, (zh * 8 + lax.rem(x + s, 4) * 2 + core, col)).start()

    @pl.loop(0, 16)
    def _(g):
        rows = dot(moves_v[0], got[pl.ds(pl.multiple_of(g * 256, 256), 256), :]).astype(BF16)
        for c in range(WIDTH):
            for h in range(CHUNKS):
                z[c, tile(g), pl.ds(h * 128, 128)] = rows[(c * 4 + h) * 16 : (c * 4 + h) * 16 + 16, :]

    convolve(z, first_v, last_v, twist_v, edge_v, tab, filt_p, skip, ends, turn, spec, resp, wave, back, conv)

    @pl.loop(0, 16)
    def _(g):
        rows = jnp.concatenate(
            [conv[c, tile(g), pl.ds(h * 128, 128)] for c in range(WIDTH) for h in range(CHUNKS)], axis=0
        )
        packed[pl.ds(pl.multiple_of(g * 256, 256), 256), :] = dot(moves_v[1], rows).astype(BF16)

    def row_tiles(index):
        return pl.ds(pl.multiple_of(index * 256, 256), 256)

    own_near = pltpu.make_async_copy(packed.at[row_tiles(row)], near.at[row_tiles(low_row)], n_recv)
    own_near.start()

    @pl.loop(1, 8)
    def _(s):
        to_row = zh * 8 + lax.rem(low_row + s, 8)
        pltpu.make_async_remote_copy(
            src_ref=packed.at[row_tiles(to_row)], dst_ref=near.at[row_tiles(low_row)],
            send_sem=n_send, recv_sem=n_recv, device_id=(to_row, col), device_id_type=MESH,
        ).start()

    @pl.loop(0, 128)
    def _(s):
        to_row = (1 - zh) * 8 + lax.rem(low_row + s // 16, 8)
        to_col = lax.rem(col + lax.rem(s, 16), 16)
        pltpu.make_async_remote_copy(
            src_ref=packed.at[tile(to_row * 16 + to_col)], dst_ref=returned.at[tile(col * 8 + low_row)],
            send_sem=b_send, recv_sem=b_recv, device_id=(to_row, to_col), device_id_type=MESH,
        ).start()

    pltpu.make_async_copy(near, near, n_recv).wait()

    @pl.loop(0, 8)
    def _(g):
        rows = jnp.concatenate([near[tile(s * 16 + g * 2 + i), :] for i in range(2) for s in range(8)], axis=0)
        rows = dot(moves_v[2], rows)
        for i in range(2):
            for h in range(CHUNKS):
                at = pl.ds(pl.multiple_of((g * 2 + i) * TOKENS + h * 128, 128), 128)
                piece = rows[i * 128 + h * 32 : i * 128 + h * 32 + 32] * near_gate[:, at].astype(F32)
                near_out[g * 2 + i, :, pl.ds(h * 128, 128)] = piece.astype(BF16)

    mine = gated.at[col, pl.ds(same, 32), :]
    own_out = pltpu.make_async_copy(near_out.at[col], mine, m_recv)
    own_out.start()

    @pl.loop(1, 16)
    def _(s):
        to_col = lax.rem(col + s, 16)
        pltpu.make_async_remote_copy(
            src_ref=near_out.at[to_col], dst_ref=mine, send_sem=m_send, recv_sem=m_recv,
            device_id=(row, to_col), device_id_type=MESH,
        ).start()

    weight_wait(w_recv, 2, w_v.at[:, :, :, pl.ds(0, 768)])
    half = w_v.at[:, :, :, pl.ds(pl.multiple_of(core * 1024, 1024), 1024)]
    weight_copy(3, half, half, (row + 1 - 2 * core, col)).start()

    pltpu.make_async_copy(gate_v, gate_v, g_recv).wait()
    pltpu.make_async_copy(returned, returned, b_recv).wait()

    @pl.loop(0, 8)
    def _(g):
        rows = dot(moves_v[2], returned[pl.ds(pl.multiple_of(g * 256, 256), 256), :])
        for i in range(2):
            for h in range(CHUNKS):
                at = pl.ds(h * 128, 128)
                piece = rows[i * 128 + h * 32 : i * 128 + h * 32 + 32] * gate_v[g * 2 + i, :, at].astype(F32)
                gated[g * 2 + i, pl.ds(cross, 32), at] = piece.astype(BF16)

    weight_wait(w_recv, 3, w_v.at[:, :, :, pl.ds(0, 1024)])
    pltpu.make_async_copy(near_out, near_out, m_recv).wait()

    @pl.loop(0, 4)
    def _(n):
        at = pl.ds(pl.multiple_of(n * 512, 512), 512)
        left = gated[...].reshape(1024, TOKENS)
        out[:, at] = dot_tn(left, w_v[:, :, :, at].reshape(1024, 512)).astype(BF16)

    pltpu.make_async_copy(sent.at[pl.ds(0, 4080)], sent.at[pl.ds(0, 4080)], a_send).wait()
    pltpu.make_async_copy(returned, returned, b_send).wait()
    pltpu.make_async_copy(gate_v.at[pl.ds(0, 15)], gate_v.at[pl.ds(0, 15)], g_send).wait()
    pltpu.make_async_copy(near.at[pl.ds(0, 1792)], near.at[pl.ds(0, 1792)], n_send).wait()
    pltpu.make_async_copy(near_out.at[pl.ds(0, 15)], near_out.at[pl.ds(0, 15)], m_send).wait()
    weight_wait(w_send, 0, w_v.at[pl.ds(0, 3), 0, :, pl.ds(0, 256)])
    weight_wait(w_send, 1, w_v.at[:, pl.ds(0, 3), :, pl.ds(0, 256)])
    weight_wait(w_send, 2, w_v.at[:, :, :, pl.ds(0, 768)])
    weight_wait(w_send, 3, w_v.at[:, :, :, pl.ds(0, 1024)])


def on_device(tokens, gate, filter_spectrum, skip_gain, kept_blocks, out_weight):
    constants = [jnp.asarray(t) for t in tables()]
    filt = jnp.transpose(filter_spectrum, (0, 3, 1, 2))
    hbm = pl.BlockSpec(memory_space=pl.ANY)
    vmem = pl.BlockSpec(memory_space=pltpu.VMEM)
    smem = pl.BlockSpec(memory_space=pltpu.SMEM)
    like = lambda t: pltpu.VMEM(t.shape, t.dtype)
    dma = pltpu.SemaphoreType.DMA
    blocks, twist, edge, first, last, pack, moves, mirror = constants
    return pl.pallas_call(
        kernel,
        out_shape=jax.ShapeDtypeStruct((TOKENS, FEATS), BF16),
        in_specs=[hbm, hbm, hbm, smem, vmem, hbm] + [hbm] * 8,
        out_specs=vmem,
        scratch_shapes=[
            like(tokens), like(filt), like(blocks), like(twist), like(edge), like(first), like(last), like(pack),
            like(moves), like(mirror),
            pltpu.VMEM((4096, 128), BF16),
            pltpu.VMEM((4096, 128), BF16),
            pltpu.VMEM((WIDTH, 256, TOKENS), BF16),
            pltpu.VMEM((2, 2 * KEPT, BLOCKS), BF16),
            pltpu.VMEM((2, WIDTH, BLOCK, KEPT), F32),
            pltpu.VMEM((8, BLOCKS), F32),
            pltpu.VMEM((2, 528, BLOCKS), BF16),
            pltpu.VMEM((528, 2 * KEPT), F32),
            pltpu.VMEM((2, 528, 2 * KEPT), BF16),
            pltpu.VMEM((528, BLOCKS), F32),
            pltpu.VMEM((2, 256, TOKENS), BF16),
            pltpu.VMEM((WIDTH, 256, TOKENS), BF16),
            pltpu.VMEM((4096, 128), BF16),
            pltpu.VMEM((2048, 128), BF16),
            pltpu.VMEM((2048, 128), BF16),
            pltpu.VMEM((32, 16 * TOKENS), BF16),
            pltpu.VMEM((16, 32, TOKENS), BF16),
            pltpu.VMEM((16, 32, TOKENS), BF16),
            pltpu.VMEM((16, 64, TOKENS), BF16),
            pltpu.VMEM((4, 4, 64, FEATS), BF16),
            dma((11,)), dma((1,)), dma, dma, dma, dma, dma((4,)), dma((4,)), dma, dma, dma, dma, dma, dma,
        ],
        compiler_params=pltpu.CompilerParams(
            collective_id=0, has_side_effects=True, vmem_limit_bytes=56 * 1024 * 1024
        ),
    )(tokens, gate.T, filt, skip_gain, kept_blocks.reshape(1, KEPT), out_weight, *constants)


def solution(mesh):
    return jax.shard_map(
        on_device,
        mesh=mesh,
        in_specs=(
            P(("row", "col"), None),
            P("row", "col"),
            P(None, None, None, ("col", "row")),
            P(("col", "row")),
            P(),
            P("col", None),
        ),
        out_specs=P(("row", "col"), None),
        check_vma=False,
    )
```

```python
import jax
import jax.numpy as jnp
import numpy as np
from jax import lax
from jax.experimental import pallas as pl
from jax.experimental.pallas import tpu as pltpu
from jax.sharding import PartitionSpec as P

SEQ = 131072
BLOCK = 128
BLOCKS = 1024
KEPT = 256
DEVICES = 256
TOKENS = SEQ // DEVICES
PAIRS = BLOCK // 2
WIDTH = 4
CHUNKS = 4
TILE = 16
FEATS = 2048
MESH = pl.DeviceIdType.MESH
BF16, F32 = jnp.bfloat16, jnp.float32


def split(table):
    high = table.astype(BF16)
    low = (table - high.astype(np.float64)).astype(BF16)
    return np.stack([high, low])


def tables():
    grid = np.arange(BLOCKS)
    angle = 2.0 * np.pi * (np.outer(2 * grid + 1, grid) % (2 * BLOCKS)) / (2 * BLOCKS)
    blocks = np.concatenate([split(np.cos(angle)), split(np.sin(angle))])
    pairs = np.arange(PAIRS)
    angle = 2.0 * np.pi * np.outer(pairs, grid) / SEQ
    cos, sin = np.cos(angle), np.sin(angle)
    masked = cos.copy()
    masked[0] = 0.0
    twist = np.stack([cos, sin, masked]).astype(np.float32)
    angle = 2.0 * np.pi * PAIRS * grid / SEQ
    edge = np.stack([np.cos(angle), np.sin(angle)]).astype(np.float32)
    j = np.arange(BLOCK)
    sign = (-1.0) ** j
    angle = 2.0 * np.pi * (np.outer(pairs, j) % BLOCK) / BLOCK
    real, imag = sign * np.cos(angle), -sign * np.sin(angle)
    imag[0] = 1.0
    first = np.zeros((2, 2, PAIRS, BLOCK, 2))
    for p in range(2):
        first[p, 0, :, :, p], first[p, 1, :, :, p] = real, imag
    first = first.reshape(256, 256)
    last = split(first.T.copy())
    first = split(first)
    pack = np.zeros((32, WIDTH, CHUNKS, CHUNKS, 32, WIDTH), np.float32)
    for o in range(32):
        for c in range(WIDTH):
            for h in range(CHUNKS):
                pack[o, c, h, h, o, c] = 1.0
    pack = pack.reshape(512, 512).astype(BF16)
    rows = np.arange(256).reshape(16, WIDTH, CHUNKS)
    eye = np.eye(256, dtype=np.float32)
    fold = eye[rows.transpose(1, 2, 0).reshape(-1)]
    rows = rows.reshape(2, 8, WIDTH, CHUNKS)
    order = eye[rows.transpose(0, 3, 1, 2).reshape(-1)]
    moves = np.stack([fold, fold.T, order]).astype(BF16)
    offsets = np.concatenate([64 + pairs, [0], 64 - pairs[1:]])
    mirror = np.eye(BLOCK, dtype=np.float32)[offsets].astype(BF16)
    return blocks, twist, edge, first, last, pack, moves, mirror


def dot(a, b):
    return lax.dot_general(a, b, (((1,), (0,)), ((), ())), preferred_element_type=F32)


def dot_nt(a, b):
    return lax.dot_general(a, b, (((1,), (1,)), ((), ())), preferred_element_type=F32)


def dot_tn(a, b):
    return lax.dot_general(a, b, (((0,), (0,)), ((), ())), preferred_element_type=F32)


def halves(value):
    high = value.astype(BF16)
    return high, (value - high.astype(F32)).astype(BF16)


def kept_table(kept, blocks):
    row = lax.broadcasted_iota(jnp.int32, (KEPT, KEPT), 0)
    lane = lax.broadcasted_iota(jnp.int32, (KEPT, KEPT), 1)
    column = jnp.sum(jnp.where(row == lane, kept.astype(F32), 0.0), axis=1, keepdims=True)
    lane = lax.broadcasted_iota(jnp.int32, (KEPT, BLOCKS), 1).astype(F32)
    pick = jnp.where(lane == column, 1.0, 0.0).astype(BF16)
    return [dot(pick, blocks[i]).astype(BF16) for i in range(4)]


def prepare(kept, blocks_v, filt_v, mirror_v, tab, filt_p):
    cos_high, cos_low, sin_high, sin_low = kept_table(kept[...], blocks_v)
    tab[0, 0:KEPT, :] = cos_high
    tab[0, KEPT:, :] = sin_high
    tab[1, 0:KEPT, :] = cos_low
    tab[1, KEPT:, :] = sin_low
    for i in range(2):
        for c in range(WIDTH):
            high, low = halves(filt_v[i, c])
            filt_p[i, c] = dot_nt(mirror_v[...], high) + dot_nt(mirror_v[...], low)


def convolve(z, first_v, last_v, twist_v, edge_v, tab, filt_p, skip, ends, turn, spec, resp, wave, back, conv):
    @pl.loop(0, WIDTH)
    def _(c):
        signal = z[c]
        spread = dot(first_v[0], signal) + dot(first_v[1], signal)
        rows = pl.ds(pl.multiple_of(c * 128, 128), 128)
        for p in range(2):
            at = pl.ds(p * TOKENS, TOKENS)
            re, im = spread[p * 128 : p * 128 + 64], spread[p * 128 + 64 : p * 128 + 128]
            cos, sin, masked = twist_v[0, :, at], twist_v[1, :, at], twist_v[2, :, at]
            both = jnp.concatenate([re * cos + im * sin, im * masked - re * sin], axis=0)
            turn[0, rows, at], turn[1, rows, at] = halves(both)
            ends[pl.ds(c, 1), at] = im[0:1]

    edge = ends[0:4, :]
    both = [edge * edge_v[0:1, :], edge * -edge_v[1:2, :], jnp.zeros((8, BLOCKS), F32)]
    turn[0, 512:528, :], turn[1, 512:528, :] = halves(jnp.concatenate(both, axis=0))

    spec[...] = dot_nt(turn[0], tab[0]) + dot_nt(turn[1], tab[0]) + dot_nt(turn[0], tab[1])

    top = lax.broadcasted_iota(jnp.int32, (PAIRS, KEPT), 0) == 0
    ends_re, ends_im = [], []
    for c in range(WIDTH):
        at = c * 128
        cos_re, sin_re = spec[at : at + 64, :KEPT], spec[at : at + 64, KEPT:]
        cos_im, sin_im = spec[at + 64 : at + 128, :KEPT], spec[at + 64 : at + 128, KEPT:]
        up_re, up_im = cos_re + sin_im, cos_im - sin_re
        edge_re = spec[512 + c : 513 + c, :KEPT] - spec[516 + c : 517 + c, KEPT:]
        edge_im = -spec[516 + c : 517 + c, :KEPT] - spec[512 + c : 513 + c, KEPT:]
        down_re = jnp.where(top, edge_re, cos_re - sin_im)
        down_im = jnp.where(top, edge_im, -cos_im - sin_re)
        filt_re, filt_im = filt_p[0, c, 0:64], filt_p[1, c, 0:64]
        up_re, up_im = filt_re * up_re - filt_im * up_im, filt_re * up_im + filt_im * up_re
        filt_re, filt_im = filt_p[0, c, 64:128], filt_p[1, c, 64:128]
        down_re, down_im = filt_re * down_re - filt_im * down_im, filt_re * down_im + filt_im * down_re
        ends_re.append(jnp.concatenate([down_re[0:1], -down_im[0:1]], axis=1))
        ends_im.append(jnp.concatenate([-down_im[0:1], -down_re[0:1]], axis=1))
        down_re, down_im = jnp.where(top, 0.0, down_re), jnp.where(top, 0.0, down_im)
        both = jnp.concatenate(
            [
                jnp.concatenate([up_re + down_re, -(up_im + down_im)], axis=1),
                jnp.concatenate([up_im - down_im, up_re - down_re], axis=1),
            ],
            axis=0,
        )
        resp[0, at : at + 128, :], resp[1, at : at + 128, :] = halves(both)
    both = jnp.concatenate(ends_re + ends_im + [jnp.zeros((8, 2 * KEPT), F32)], axis=0)
    resp[0, 512:528, :], resp[1, 512:528, :] = halves(both)

    wave[...] = dot(resp[0], tab[0]) + dot(resp[1], tab[0]) + dot(resp[0], tab[1])
    edge = wave[512:516, :] * edge_v[0:1, :] - wave[516:520, :] * edge_v[1:2, :]
    ends[0:4, :] = edge

    @pl.loop(0, WIDTH)
    def _(c):
        top = lax.broadcasted_iota(jnp.int32, (PAIRS, TOKENS), 0) == 0
        start = pl.multiple_of(c * 128, 128)
        for p in range(2):
            at = pl.ds(p * TOKENS, TOKENS)
            re, im = wave[pl.ds(start, 64), at], wave[pl.ds(start + 64, 64), at]
            cos, sin = twist_v[0, :, at], twist_v[1, :, at]
            low = jnp.where(top, ends[pl.ds(c, 1), at], im * cos + re * sin)
            both = jnp.concatenate([re * cos - im * sin, low], axis=0)
            back[0, p * 128 : p * 128 + 128, :], back[1, p * 128 : p * 128 + 128, :] = halves(both)
        result = dot(last_v[0], back[0]) + dot(last_v[1], back[0]) + dot(last_v[0], back[1])
        conv[c] = (result * (1.0 / SEQ) + skip[c] * z[c].astype(F32)).astype(BF16)


def kernel(
    tokens, gate, filt, skip, kept, weight, blocks, twist, edge, first, last, pack, moves, mirror,
    out,
    tok_v, filt_v, blocks_v, twist_v, edge_v, first_v, last_v, pack_v, moves_v, mirror_v,
    sent, got, z, tab, filt_p, ends, turn, spec, resp, wave, back, conv, packed, returned, near, near_gate, near_out,
    gate_v, gated, w_v,
    local, own, a_send, a_recv, g_send, g_recv, w_send, w_recv, b_send, b_recv, n_send, n_recv, m_send, m_recv,
):
    row, col = lax.axis_index("row"), lax.axis_index("col")
    zh, x, core = row // 8, lax.rem(row, 8) // 2, lax.rem(row, 2)
    low_row = lax.rem(row, 8)
    zl, y = col // 4, lax.rem(col, 4)
    as_tokens, as_channels = row * 16 + col, col * 16 + row

    barrier = pltpu.get_barrier_semaphore()

    @pl.loop(1, DEVICES)
    def _(s):
        other = (lax.rem(row + s // 16, 16), lax.rem(col + lax.rem(s, 16), 16))
        pl.semaphore_signal(barrier, inc=1, device_id=other, device_id_type=MESH)

    same = pl.multiple_of(zh * 32, 32)
    cross = pl.multiple_of(32 - zh * 32, 32)
    loads = [
        pltpu.make_async_copy(src, dst, local.at[i])
        for i, (src, dst) in enumerate(
            [(tokens, tok_v), (pack, pack_v), (blocks, blocks_v), (moves, moves_v), (first, first_v),
             (twist, twist_v), (last, last_v), (edge, edge_v), (mirror, mirror_v),
             (gate.at[pl.ds(same, 32), :], near_gate)]
            + [(filt.at[i, :, c, :], filt_v.at[i, c]) for i in range(2) for c in range(WIDTH)]
        )
    ]
    for load in loads:
        load.start()

    def columns(part, width):
        return pl.ds(pl.multiple_of(core * 1024 + part * 128, 128), width)

    slices = [columns(x, 128), columns(4 + x, 128)]
    own_weight = [
        pltpu.make_async_copy(weight.at[:, at], w_v.at[zl, y, :, at], own.at[i]) for i, at in enumerate(slices)
    ]
    for load in own_weight:
        load.start()

    loads[0].wait()
    loads[1].wait()

    @pl.loop(0, 8)
    def _(g):
        at = pl.ds(pl.multiple_of(g * 128, 128), 128)
        wide = jnp.concatenate([tok_v[pl.ds(h * 128, 128), at] for h in range(CHUNKS)], axis=1)
        sent[pl.ds(pl.multiple_of(g * 512, 512), 512), :] = dot_nt(pack_v[...], wide).astype(BF16)

    pl.semaphore_wait(barrier, DEVICES - 1)

    def tile(index):
        return pl.ds(pl.multiple_of(index * TILE, TILE), TILE)

    def weight_copy(stage, src, dst, device):
        return pltpu.make_async_remote_copy(
            src_ref=src, dst_ref=dst, send_sem=w_send.at[stage], recv_sem=w_recv.at[stage],
            device_id=device, device_id_type=MESH,
        )

    for s in range(1, 4):
        for at in slices:
            weight_copy(0, weight.at[:, at], w_v.at[zl, y, :, at], (row, lax.rem(zl + s, 4) * 4 + y)).start()

    own_tile = pltpu.make_async_copy(sent.at[tile(as_channels)], got.at[tile(as_tokens)], a_recv)
    own_tile.start()

    @pl.loop(1, DEVICES)
    def _(s):
        to_row, to_col = lax.rem(row + s // 16, 16), lax.rem(col + lax.rem(s, 16), 16)
        pltpu.make_async_remote_copy(
            src_ref=sent.at[tile(to_col * 16 + to_row)], dst_ref=got.at[tile(as_tokens)],
            send_sem=a_send, recv_sem=a_recv, device_id=(to_row, to_col), device_id_type=MESH,
        ).start()

    def at_x(other):
        return (zh * 8 + lax.rem(other + 4, 4) * 2 + core, col)

    def at_y(other):
        return (row, zl * 4 + lax.rem(other + 4, 4))

    for load in loads[2:]:
        load.wait()
    prepare(kept, blocks_v, filt_v, mirror_v, tab, filt_p)

    def weight_wait(sem, stage, ref):
        pltpu.make_async_copy(ref, ref, sem.at[stage]).wait()

    for load in own_weight:
        load.wait()
    weight_wait(w_recv, 0, w_v.at[0, pl.ds(0, 3), :, pl.ds(0, 256)])
    for s in range(1, 4):
        part = w_v.at[:, y, :, slices[0]]
        weight_copy(1, part, part, at_y(y + s)).start()
        part = w_v.at[:, y, :, slices[1]]
        weight_copy(1, part, part, at_x(x + s)).start()

    pltpu.make_async_copy(got, got, a_recv).wait()

    def gate_at(to_col):
        return gate.at[pl.ds(cross, 32), pl.ds(pl.multiple_of(to_col * TOKENS, TOKENS), TOKENS)]

    own_gate = pltpu.make_async_copy(gate_at(col), gate_v.at[col], g_recv)
    own_gate.start()

    @pl.loop(1, 16)
    def _(s):
        to_col = lax.rem(col + s, 16)
        pltpu.make_async_remote_copy(
            src_ref=gate_at(to_col), dst_ref=gate_v.at[col], send_sem=g_send, recv_sem=g_recv,
            device_id=(row, to_col), device_id_type=MESH,
        ).start()

    weight_wait(w_recv, 1, w_v.at[:, pl.ds(0, 3), :, pl.ds(0, 256)])
    for step in (1, -1):
        part = w_v.at[:, :, :, slices[0]]
        weight_copy(2, part, part, at_x(x + step)).start()
        part = w_v.at[:, y, :, columns(4, 512)]
        weight_copy(2, part, part, at_y(y + step)).start()

    @pl.loop(0, 16)
    def _(g):
        rows = dot(moves_v[0], got[pl.ds(pl.multiple_of(g * 256, 256), 256), :]).astype(BF16)
        for c in range(WIDTH):
            for h in range(CHUNKS):
                z[c, tile(g), pl.ds(h * 128, 128)] = rows[(c * 4 + h) * 16 : (c * 4 + h) * 16 + 16, :]

    convolve(z, first_v, last_v, twist_v, edge_v, tab, filt_p, skip, ends, turn, spec, resp, wave, back, conv)

    @pl.loop(0, 16)
    def _(g):
        rows = jnp.concatenate(
            [conv[c, tile(g), pl.ds(h * 128, 128)] for c in range(WIDTH) for h in range(CHUNKS)], axis=0
        )
        packed[pl.ds(pl.multiple_of(g * 256, 256), 256), :] = dot(moves_v[1], rows).astype(BF16)

    def row_tiles(index):
        return pl.ds(pl.multiple_of(index * 256, 256), 256)

    own_near = pltpu.make_async_copy(packed.at[row_tiles(row)], near.at[row_tiles(low_row)], n_recv)
    own_near.start()

    @pl.loop(1, 8)
    def _(s):
        to_row = zh * 8 + lax.rem(low_row + s, 8)
        pltpu.make_async_remote_copy(
            src_ref=packed.at[row_tiles(to_row)], dst_ref=near.at[row_tiles(low_row)],
            send_sem=n_send, recv_sem=n_recv, device_id=(to_row, col), device_id_type=MESH,
        ).start()

    weight_wait(w_recv, 2, w_v.at[:, :, :, pl.ds(0, 512)])
    for step, rows in ((1, pl.ds(0, 2)), (-1, pl.ds(2, 2))):
        part = w_v.at[rows, :, :, columns(lax.rem(x - step + 4, 4), 128)]
        weight_copy(3, part, part, at_x(x + step)).start()
        part = w_v.at[rows, lax.rem(y - step + 4, 4), :, columns(4, 512)]
        weight_copy(3, part, part, at_y(y + step)).start()

    @pl.loop(0, 128)
    def _(s):
        to_row = (1 - zh) * 8 + lax.rem(low_row + s // 16, 8)
        to_col = lax.rem(col + lax.rem(s, 16), 16)
        pltpu.make_async_remote_copy(
            src_ref=packed.at[tile(to_row * 16 + to_col)], dst_ref=returned.at[tile(col * 8 + low_row)],
            send_sem=b_send, recv_sem=b_recv, device_id=(to_row, to_col), device_id_type=MESH,
        ).start()

    pltpu.make_async_copy(near, near, n_recv).wait()

    @pl.loop(0, 8)
    def _(g):
        rows = jnp.concatenate([near[tile(s * 16 + g * 2 + i), :] for i in range(2) for s in range(8)], axis=0)
        rows = dot(moves_v[2], rows)
        for i in range(2):
            for h in range(CHUNKS):
                at = pl.ds(pl.multiple_of((g * 2 + i) * TOKENS + h * 128, 128), 128)
                piece = rows[i * 128 + h * 32 : i * 128 + h * 32 + 32] * near_gate[:, at].astype(F32)
                near_out[g * 2 + i, :, pl.ds(h * 128, 128)] = piece.astype(BF16)

    mine = gated.at[col, pl.ds(same, 32), :]
    own_out = pltpu.make_async_copy(near_out.at[col], mine, m_recv)
    own_out.start()

    @pl.loop(1, 16)
    def _(s):
        to_col = lax.rem(col + s, 16)
        pltpu.make_async_remote_copy(
            src_ref=near_out.at[to_col], dst_ref=mine, send_sem=m_send, recv_sem=m_recv,
            device_id=(row, to_col), device_id_type=MESH,
        ).start()

    weight_wait(w_recv, 3, w_v.at[:, :, :, pl.ds(0, 256)])
    half = w_v.at[:, :, :, columns(0, 1024)]
    weight_copy(4, half, half, (row + 1 - 2 * core, col)).start()

    pltpu.make_async_copy(gate_v, gate_v, g_recv).wait()
    pltpu.make_async_copy(returned, returned, b_recv).wait()

    @pl.loop(0, 8)
    def _(g):
        rows = dot(moves_v[2], returned[pl.ds(pl.multiple_of(g * 256, 256), 256), :])
        for i in range(2):
            for h in range(CHUNKS):
                at = pl.ds(h * 128, 128)
                piece = rows[i * 128 + h * 32 : i * 128 + h * 32 + 32] * gate_v[g * 2 + i, :, at].astype(F32)
                gated[g * 2 + i, pl.ds(cross, 32), at] = piece.astype(BF16)

    weight_wait(w_recv, 4, w_v.at[:, :, :, pl.ds(0, 1024)])
    pltpu.make_async_copy(near_out, near_out, m_recv).wait()

    @pl.loop(0, 4)
    def _(n):
        at = pl.ds(pl.multiple_of(n * 512, 512), 512)
        left = gated[...].reshape(1024, TOKENS)
        out[:, at] = dot_tn(left, w_v[:, :, :, at].reshape(1024, 512)).astype(BF16)

    pltpu.make_async_copy(sent.at[pl.ds(0, 4080)], sent.at[pl.ds(0, 4080)], a_send).wait()
    pltpu.make_async_copy(returned, returned, b_send).wait()
    pltpu.make_async_copy(gate_v.at[pl.ds(0, 15)], gate_v.at[pl.ds(0, 15)], g_send).wait()
    pltpu.make_async_copy(near.at[pl.ds(0, 1792)], near.at[pl.ds(0, 1792)], n_send).wait()
    pltpu.make_async_copy(near_out.at[pl.ds(0, 15)], near_out.at[pl.ds(0, 15)], m_send).wait()
    weight_wait(w_send, 0, w_v.at[0, pl.ds(0, 3), :, pl.ds(0, 256)])
    weight_wait(w_send, 1, w_v.at[:, pl.ds(0, 3), :, pl.ds(0, 256)])
    weight_wait(w_send, 2, w_v.at[:, :, :, pl.ds(0, 512)])
    weight_wait(w_send, 3, w_v.at[:, :, :, pl.ds(0, 256)])
    weight_wait(w_send, 4, w_v.at[:, :, :, pl.ds(0, 1024)])


def on_device(tokens, gate, filter_spectrum, skip_gain, kept_blocks, out_weight):
    constants = [jnp.asarray(t) for t in tables()]
    filt = jnp.transpose(filter_spectrum, (0, 1, 3, 2))
    hbm = pl.BlockSpec(memory_space=pl.ANY)
    vmem = pl.BlockSpec(memory_space=pltpu.VMEM)
    smem = pl.BlockSpec(memory_space=pltpu.SMEM)
    like = lambda t: pltpu.VMEM(t.shape, t.dtype)
    dma = pltpu.SemaphoreType.DMA
    blocks, twist, edge, first, last, pack, moves, mirror = constants
    return pl.pallas_call(
        kernel,
        out_shape=pltpu.VMEM((TOKENS, FEATS), BF16),
        in_specs=[hbm, hbm, hbm, smem, vmem, hbm] + [hbm] * 8,
        out_specs=vmem,
        scratch_shapes=[
            like(tokens), pltpu.VMEM((2, WIDTH, KEPT, BLOCK), F32), like(blocks), like(twist), like(edge), like(first), like(last), like(pack),
            like(moves), like(mirror),
            pltpu.VMEM((4096, 128), BF16),
            pltpu.VMEM((4096, 128), BF16),
            pltpu.VMEM((WIDTH, 256, TOKENS), BF16),
            pltpu.VMEM((2, 2 * KEPT, BLOCKS), BF16),
            pltpu.VMEM((2, WIDTH, BLOCK, KEPT), F32),
            pltpu.VMEM((8, BLOCKS), F32),
            pltpu.VMEM((2, 528, BLOCKS), BF16),
            pltpu.VMEM((528, 2 * KEPT), F32),
            pltpu.VMEM((2, 528, 2 * KEPT), BF16),
            pltpu.VMEM((528, BLOCKS), F32),
            pltpu.VMEM((2, 256, TOKENS), BF16),
            pltpu.VMEM((WIDTH, 256, TOKENS), BF16),
            pltpu.VMEM((4096, 128), BF16),
            pltpu.VMEM((2048, 128), BF16),
            pltpu.VMEM((2048, 128), BF16),
            pltpu.VMEM((32, 16 * TOKENS), BF16),
            pltpu.VMEM((16, 32, TOKENS), BF16),
            pltpu.VMEM((16, 32, TOKENS), BF16),
            pltpu.VMEM((16, 64, TOKENS), BF16),
            pltpu.VMEM((4, 4, 64, FEATS), BF16),
            dma((18,)), dma((2,)), dma, dma, dma, dma, dma((5,)), dma((5,)), dma, dma, dma, dma, dma, dma,
        ],
        compiler_params=pltpu.CompilerParams(
            collective_id=0, has_side_effects=True, vmem_limit_bytes=56 * 1024 * 1024
        ),
    )(tokens, gate.T, filt, skip_gain, kept_blocks.reshape(1, KEPT), out_weight, *constants)


def solution(mesh):
    return jax.shard_map(
        on_device,
        mesh=mesh,
        in_specs=(
            P(("row", "col"), None),
            P("row", "col"),
            P(None, None, None, ("col", "row")),
            P(("col", "row")),
            P(),
            P("col", None),
        ),
        out_specs=P(("row", "col"), None),
        check_vma=False,
    )
```

```python
import jax
import jax.numpy as jnp
import numpy as np
from jax import lax
from jax.experimental import pallas as pl
from jax.experimental.pallas import tpu as pltpu
from jax.sharding import PartitionSpec as P

SEQ = 131072
BLOCK = 128
BLOCKS = 1024
KEPT = 256
DEVICES = 256
TOKENS = SEQ // DEVICES
PAIRS = BLOCK // 2
WIDTH = 4
CHUNKS = 4
TILE = 16
FEATS = 2048
MESH = pl.DeviceIdType.MESH
BF16, F32 = jnp.bfloat16, jnp.float32


def split(table):
    high = table.astype(BF16)
    low = (table - high.astype(np.float64)).astype(BF16)
    return np.stack([high, low])


def tables():
    grid = np.arange(BLOCKS)
    angle = 2.0 * np.pi * (np.outer(2 * grid + 1, grid) % (2 * BLOCKS)) / (2 * BLOCKS)
    blocks = np.concatenate([split(np.cos(angle)), split(np.sin(angle))])
    pairs = np.arange(PAIRS)
    angle = 2.0 * np.pi * np.outer(pairs, grid) / SEQ
    cos, sin = np.cos(angle), np.sin(angle)
    masked = cos.copy()
    masked[0] = 0.0
    twist = np.stack([cos, sin, masked]).astype(np.float32)
    angle = 2.0 * np.pi * PAIRS * grid / SEQ
    edge = np.stack([np.cos(angle), np.sin(angle)]).astype(np.float32)
    j = np.arange(BLOCK)
    sign = (-1.0) ** j
    angle = 2.0 * np.pi * (np.outer(pairs, j) % BLOCK) / BLOCK
    real, imag = sign * np.cos(angle), -sign * np.sin(angle)
    imag[0] = 1.0
    first = np.zeros((2, 2, PAIRS, BLOCK, 2))
    for p in range(2):
        first[p, 0, :, :, p], first[p, 1, :, :, p] = real, imag
    first = first.reshape(256, 256)
    last = split(first.T.copy())
    first = split(first)
    pack = np.zeros((32, WIDTH, CHUNKS, CHUNKS, 32, WIDTH), np.float32)
    for o in range(32):
        for c in range(WIDTH):
            for h in range(CHUNKS):
                pack[o, c, h, h, o, c] = 1.0
    pack = pack.reshape(512, 512).astype(BF16)
    rows = np.arange(256).reshape(16, WIDTH, CHUNKS)
    eye = np.eye(256, dtype=np.float32)
    fold = eye[rows.transpose(1, 2, 0).reshape(-1)]
    rows = rows.reshape(2, 8, WIDTH, CHUNKS)
    order = eye[rows.transpose(0, 3, 1, 2).reshape(-1)]
    moves = np.stack([fold, fold.T, order]).astype(BF16)
    offsets = np.concatenate([64 + pairs, [0], 64 - pairs[1:]])
    mirror = np.eye(BLOCK, dtype=np.float32)[offsets].astype(BF16)
    return blocks, twist, edge, first, last, pack, moves, mirror


def dot(a, b):
    return lax.dot_general(a, b, (((1,), (0,)), ((), ())), preferred_element_type=F32)


def dot_nt(a, b):
    return lax.dot_general(a, b, (((1,), (1,)), ((), ())), preferred_element_type=F32)


def dot_tn(a, b):
    return lax.dot_general(a, b, (((0,), (0,)), ((), ())), preferred_element_type=F32)


def halves(value):
    high = value.astype(BF16)
    return high, (value - high.astype(F32)).astype(BF16)


def kept_table(kept, blocks):
    row = lax.broadcasted_iota(jnp.int32, (KEPT, KEPT), 0)
    lane = lax.broadcasted_iota(jnp.int32, (KEPT, KEPT), 1)
    column = jnp.sum(jnp.where(row == lane, kept.astype(F32), 0.0), axis=1, keepdims=True)
    lane = lax.broadcasted_iota(jnp.int32, (KEPT, BLOCKS), 1).astype(F32)
    pick = jnp.where(lane == column, 1.0, 0.0).astype(BF16)
    return [dot(pick, blocks[i]).astype(BF16) for i in range(4)]


def prepare(kept, blocks_v, filt_v, mirror_v, tab, filt_p):
    cos_high, cos_low, sin_high, sin_low = kept_table(kept[...], blocks_v)
    tab[0, 0:KEPT, :] = cos_high
    tab[0, KEPT:, :] = sin_high
    tab[1, 0:KEPT, :] = cos_low
    tab[1, KEPT:, :] = sin_low
    for i in range(2):
        for c in range(WIDTH):
            high, low = halves(filt_v[i, c])
            filt_p[i, c] = dot_nt(mirror_v[...], high) + dot_nt(mirror_v[...], low)


def convolve(z, first_v, last_v, twist_v, edge_v, tab, filt_p, skip, ends, turn, spec, resp, wave, back, conv):
    @pl.loop(0, WIDTH)
    def _(c):
        signal = z[c]
        spread = dot(first_v[0], signal) + dot(first_v[1], signal)
        rows = pl.ds(pl.multiple_of(c * 128, 128), 128)
        for p in range(2):
            at = pl.ds(p * TOKENS, TOKENS)
            re, im = spread[p * 128 : p * 128 + 64], spread[p * 128 + 64 : p * 128 + 128]
            cos, sin, masked = twist_v[0, :, at], twist_v[1, :, at], twist_v[2, :, at]
            both = jnp.concatenate([re * cos + im * sin, im * masked - re * sin], axis=0)
            turn[0, rows, at], turn[1, rows, at] = halves(both)
            ends[pl.ds(c, 1), at] = im[0:1]

    edge = ends[0:4, :]
    both = [edge * edge_v[0:1, :], edge * -edge_v[1:2, :], jnp.zeros((8, BLOCKS), F32)]
    turn[0, 512:528, :], turn[1, 512:528, :] = halves(jnp.concatenate(both, axis=0))

    spec[...] = dot_nt(turn[0], tab[0]) + dot_nt(turn[1], tab[0]) + dot_nt(turn[0], tab[1])

    top = lax.broadcasted_iota(jnp.int32, (PAIRS, KEPT), 0) == 0
    ends_re, ends_im = [], []
    for c in range(WIDTH):
        at = c * 128
        cos_re, sin_re = spec[at : at + 64, :KEPT], spec[at : at + 64, KEPT:]
        cos_im, sin_im = spec[at + 64 : at + 128, :KEPT], spec[at + 64 : at + 128, KEPT:]
        up_re, up_im = cos_re + sin_im, cos_im - sin_re
        edge_re = spec[512 + c : 513 + c, :KEPT] - spec[516 + c : 517 + c, KEPT:]
        edge_im = -spec[516 + c : 517 + c, :KEPT] - spec[512 + c : 513 + c, KEPT:]
        down_re = jnp.where(top, edge_re, cos_re - sin_im)
        down_im = jnp.where(top, edge_im, -cos_im - sin_re)
        filt_re, filt_im = filt_p[0, c, 0:64], filt_p[1, c, 0:64]
        up_re, up_im = filt_re * up_re - filt_im * up_im, filt_re * up_im + filt_im * up_re
        filt_re, filt_im = filt_p[0, c, 64:128], filt_p[1, c, 64:128]
        down_re, down_im = filt_re * down_re - filt_im * down_im, filt_re * down_im + filt_im * down_re
        ends_re.append(jnp.concatenate([down_re[0:1], -down_im[0:1]], axis=1))
        ends_im.append(jnp.concatenate([-down_im[0:1], -down_re[0:1]], axis=1))
        down_re, down_im = jnp.where(top, 0.0, down_re), jnp.where(top, 0.0, down_im)
        both = jnp.concatenate(
            [
                jnp.concatenate([up_re + down_re, -(up_im + down_im)], axis=1),
                jnp.concatenate([up_im - down_im, up_re - down_re], axis=1),
            ],
            axis=0,
        )
        resp[0, at : at + 128, :], resp[1, at : at + 128, :] = halves(both)
    both = jnp.concatenate(ends_re + ends_im + [jnp.zeros((8, 2 * KEPT), F32)], axis=0)
    resp[0, 512:528, :], resp[1, 512:528, :] = halves(both)

    wave[...] = dot(resp[0], tab[0]) + dot(resp[1], tab[0]) + dot(resp[0], tab[1])
    edge = wave[512:516, :] * edge_v[0:1, :] - wave[516:520, :] * edge_v[1:2, :]
    ends[0:4, :] = edge

    @pl.loop(0, WIDTH)
    def _(c):
        top = lax.broadcasted_iota(jnp.int32, (PAIRS, TOKENS), 0) == 0
        start = pl.multiple_of(c * 128, 128)
        for p in range(2):
            at = pl.ds(p * TOKENS, TOKENS)
            re, im = wave[pl.ds(start, 64), at], wave[pl.ds(start + 64, 64), at]
            cos, sin = twist_v[0, :, at], twist_v[1, :, at]
            low = jnp.where(top, ends[pl.ds(c, 1), at], im * cos + re * sin)
            both = jnp.concatenate([re * cos - im * sin, low], axis=0)
            back[0, p * 128 : p * 128 + 128, :], back[1, p * 128 : p * 128 + 128, :] = halves(both)
        result = dot(last_v[0], back[0]) + dot(last_v[1], back[0]) + dot(last_v[0], back[1])
        conv[c] = (result * (1.0 / SEQ) + skip[c] * z[c].astype(F32)).astype(BF16)


def kernel(
    tokens, gate, filt, skip, kept, weight, blocks, twist, edge, first, last, pack, moves, mirror,
    out,
    tok_v, filt_v, blocks_v, twist_v, edge_v, first_v, last_v, pack_v, moves_v, mirror_v,
    sent, got, z, tab, filt_p, ends, turn, spec, resp, wave, back, conv, packed, returned, near, near_gate, near_out,
    gate_v, gated, w_v,
    local, own, a_send, a_recv, g_send, g_recv, w_send, w_recv, b_send, b_recv, n_send, n_recv, m_send, m_recv,
):
    row, col = lax.axis_index("row"), lax.axis_index("col")
    zh, x, core = row // 8, lax.rem(row, 8) // 2, lax.rem(row, 2)
    low_row = lax.rem(row, 8)
    zl, y = col // 4, lax.rem(col, 4)
    as_tokens, as_channels = row * 16 + col, col * 16 + row

    same = pl.multiple_of(zh * 32, 32)
    cross = pl.multiple_of(32 - zh * 32, 32)
    loads = [
        pltpu.make_async_copy(src, dst, local.at[i])
        for i, (src, dst) in enumerate(
            [(tokens, tok_v), (pack, pack_v), (blocks, blocks_v), (moves, moves_v), (first, first_v),
             (twist, twist_v), (last, last_v), (edge, edge_v), (mirror, mirror_v),
             (gate.at[pl.ds(same, 32), :], near_gate)]
            + [(filt.at[i, :, c, :], filt_v.at[i, c]) for i in range(2) for c in range(WIDTH)]
        )
    ]
    for load in loads[:2]:
        load.start()

    barrier = pltpu.get_barrier_semaphore()

    columns_on = [lax.rem(col + i, 16) for i in range(16)]

    def greet(to_row, steps):
        for i in steps:
            pl.semaphore_signal(barrier, inc=1, device_id=(to_row, columns_on[i]), device_id_type=MESH)

    greet(row, range(1, 16))

    @pl.loop(1, 16)
    def _(s):
        greet(lax.rem(row + s, 16), range(16))

    def columns(part, width):
        return pl.ds(pl.multiple_of(core * 1024 + part * 128, 128), width)

    slices = [columns(x, 128), columns(4 + x, 128)]
    own_weight = [
        pltpu.make_async_copy(weight.at[:, at], w_v.at[zl, y, :, at], own.at[i]) for i, at in enumerate(slices)
    ]
    for load in own_weight:
        load.start()

    loads[0].wait()
    loads[1].wait()

    @pl.loop(0, 8)
    def _(g):
        at = pl.ds(pl.multiple_of(g * 128, 128), 128)
        wide = jnp.concatenate([tok_v[pl.ds(h * 128, 128), at] for h in range(CHUNKS)], axis=1)
        sent[pl.ds(pl.multiple_of(g * 512, 512), 512), :] = dot_nt(pack_v[...], wide).astype(BF16)

    pl.semaphore_wait(barrier, DEVICES - 1)

    def tile(index):
        return pl.ds(pl.multiple_of(index * TILE, TILE), TILE)

    def weight_copy(stage, src, dst, device):
        return pltpu.make_async_remote_copy(
            src_ref=src, dst_ref=dst, send_sem=w_send.at[stage], recv_sem=w_recv.at[stage],
            device_id=device, device_id_type=MESH,
        )

    for s in range(1, 4):
        for at in slices:
            weight_copy(0, weight.at[:, at], w_v.at[zl, y, :, at], (row, lax.rem(zl + s, 4) * 4 + y)).start()

    own_tile = pltpu.make_async_copy(sent.at[tile(as_channels)], got.at[tile(as_tokens)], a_recv)
    own_tile.start()

    def send_tokens(to_row, steps):
        for i in steps:
            pltpu.make_async_remote_copy(
                src_ref=sent.at[tile(columns_on[i] * 16 + to_row)], dst_ref=got.at[tile(as_tokens)],
                send_sem=a_send, recv_sem=a_recv, device_id=(to_row, columns_on[i]), device_id_type=MESH,
            ).start()

    send_tokens(row, range(1, 16))

    @pl.loop(1, 16)
    def _(s):
        send_tokens(lax.rem(row + s, 16), range(16))

    for load in loads[2:]:
        load.start()
    def at_x(other):
        return (zh * 8 + lax.rem(other + 4, 4) * 2 + core, col)

    def at_y(other):
        return (row, zl * 4 + lax.rem(other + 4, 4))

    for load in loads[2:]:
        load.wait()
    prepare(kept, blocks_v, filt_v, mirror_v, tab, filt_p)

    def weight_wait(sem, stage, ref):
        pltpu.make_async_copy(ref, ref, sem.at[stage]).wait()

    for load in own_weight:
        load.wait()
    weight_wait(w_recv, 0, w_v.at[0, pl.ds(0, 3), :, pl.ds(0, 256)])
    for s in range(1, 4):
        part = w_v.at[:, y, :, slices[0]]
        weight_copy(1, part, part, at_y(y + s)).start()
        part = w_v.at[:, y, :, slices[1]]
        weight_copy(1, part, part, at_x(x + s)).start()

    pltpu.make_async_copy(got, got, a_recv).wait()

    def gate_at(to_col):
        return gate.at[pl.ds(cross, 32), pl.ds(pl.multiple_of(to_col * TOKENS, TOKENS), TOKENS)]

    own_gate = pltpu.make_async_copy(gate_at(col), gate_v.at[col], g_recv)
    own_gate.start()

    @pl.loop(1, 16)
    def _(s):
        to_col = lax.rem(col + s, 16)
        pltpu.make_async_remote_copy(
            src_ref=gate_at(to_col), dst_ref=gate_v.at[col], send_sem=g_send, recv_sem=g_recv,
            device_id=(row, to_col), device_id_type=MESH,
        ).start()

    weight_wait(w_recv, 1, w_v.at[:, pl.ds(0, 3), :, pl.ds(0, 256)])
    for step in (1, -1):
        part = w_v.at[:, :, :, slices[0]]
        weight_copy(2, part, part, at_x(x + step)).start()
        part = w_v.at[:, y, :, columns(4, 512)]
        weight_copy(2, part, part, at_y(y + step)).start()

    @pl.loop(0, 16)
    def _(g):
        rows = dot(moves_v[0], got[pl.ds(pl.multiple_of(g * 256, 256), 256), :]).astype(BF16)
        for c in range(WIDTH):
            for h in range(CHUNKS):
                z[c, tile(g), pl.ds(h * 128, 128)] = rows[(c * 4 + h) * 16 : (c * 4 + h) * 16 + 16, :]

    convolve(z, first_v, last_v, twist_v, edge_v, tab, filt_p, skip, ends, turn, spec, resp, wave, back, conv)

    @pl.loop(0, 16)
    def _(g):
        rows = jnp.concatenate(
            [conv[c, tile(g), pl.ds(h * 128, 128)] for c in range(WIDTH) for h in range(CHUNKS)], axis=0
        )
        packed[pl.ds(pl.multiple_of(g * 256, 256), 256), :] = dot(moves_v[1], rows).astype(BF16)

    def row_tiles(index):
        return pl.ds(pl.multiple_of(index * 256, 256), 256)

    own_near = pltpu.make_async_copy(packed.at[row_tiles(row)], near.at[row_tiles(low_row)], n_recv)
    own_near.start()

    @pl.loop(1, 8)
    def _(s):
        to_row = zh * 8 + lax.rem(low_row + s, 8)
        pltpu.make_async_remote_copy(
            src_ref=packed.at[row_tiles(to_row)], dst_ref=near.at[row_tiles(low_row)],
            send_sem=n_send, recv_sem=n_recv, device_id=(to_row, col), device_id_type=MESH,
        ).start()

    weight_wait(w_recv, 2, w_v.at[:, :, :, pl.ds(0, 512)])
    for step, rows in ((1, pl.ds(0, 2)), (-1, pl.ds(2, 2))):
        part = w_v.at[rows, :, :, columns(lax.rem(x - step + 4, 4), 128)]
        weight_copy(3, part, part, at_x(x + step)).start()
        part = w_v.at[rows, lax.rem(y - step + 4, 4), :, columns(4, 512)]
        weight_copy(3, part, part, at_y(y + step)).start()

    @pl.loop(0, 8)
    def _(s):
        to_row = (1 - zh) * 8 + lax.rem(low_row + s, 8)
        for to_col in columns_on:
            pltpu.make_async_remote_copy(
                src_ref=packed.at[tile(to_row * 16 + to_col)], dst_ref=returned.at[tile(col * 8 + low_row)],
                send_sem=b_send, recv_sem=b_recv, device_id=(to_row, to_col), device_id_type=MESH,
            ).start()

    pltpu.make_async_copy(near, near, n_recv).wait()

    @pl.loop(0, 8)
    def _(g):
        rows = jnp.concatenate([near[tile(s * 16 + g * 2 + i), :] for i in range(2) for s in range(8)], axis=0)
        rows = dot(moves_v[2], rows)
        for i in range(2):
            for h in range(CHUNKS):
                at = pl.ds(pl.multiple_of((g * 2 + i) * TOKENS + h * 128, 128), 128)
                piece = rows[i * 128 + h * 32 : i * 128 + h * 32 + 32] * near_gate[:, at].astype(F32)
                near_out[g * 2 + i, :, pl.ds(h * 128, 128)] = piece.astype(BF16)

    mine = gated.at[col, pl.ds(same, 32), :]
    own_out = pltpu.make_async_copy(near_out.at[col], mine, m_recv)
    own_out.start()

    @pl.loop(1, 16)
    def _(s):
        to_col = lax.rem(col + s, 16)
        pltpu.make_async_remote_copy(
            src_ref=near_out.at[to_col], dst_ref=mine, send_sem=m_send, recv_sem=m_recv,
            device_id=(row, to_col), device_id_type=MESH,
        ).start()

    weight_wait(w_recv, 3, w_v.at[:, :, :, pl.ds(0, 256)])
    half = w_v.at[:, :, :, columns(0, 1024)]
    weight_copy(4, half, half, (row + 1 - 2 * core, col)).start()

    pltpu.make_async_copy(gate_v, gate_v, g_recv).wait()
    pltpu.make_async_copy(returned, returned, b_recv).wait()

    @pl.loop(0, 8)
    def _(g):
        rows = dot(moves_v[2], returned[pl.ds(pl.multiple_of(g * 256, 256), 256), :])
        for i in range(2):
            for h in range(CHUNKS):
                at = pl.ds(h * 128, 128)
                piece = rows[i * 128 + h * 32 : i * 128 + h * 32 + 32] * gate_v[g * 2 + i, :, at].astype(F32)
                gated[g * 2 + i, pl.ds(cross, 32), at] = piece.astype(BF16)

    weight_wait(w_recv, 4, w_v.at[:, :, :, pl.ds(0, 1024)])
    pltpu.make_async_copy(near_out, near_out, m_recv).wait()

    @pl.loop(0, 4)
    def _(n):
        at = pl.ds(pl.multiple_of(n * 512, 512), 512)
        left = gated[...].reshape(1024, TOKENS)
        out[:, at] = dot_tn(left, w_v[:, :, :, at].reshape(1024, 512)).astype(BF16)

    pltpu.make_async_copy(sent.at[pl.ds(0, 4080)], sent.at[pl.ds(0, 4080)], a_send).wait()
    pltpu.make_async_copy(returned, returned, b_send).wait()
    pltpu.make_async_copy(gate_v.at[pl.ds(0, 15)], gate_v.at[pl.ds(0, 15)], g_send).wait()
    pltpu.make_async_copy(near.at[pl.ds(0, 1792)], near.at[pl.ds(0, 1792)], n_send).wait()
    pltpu.make_async_copy(near_out.at[pl.ds(0, 15)], near_out.at[pl.ds(0, 15)], m_send).wait()
    weight_wait(w_send, 0, w_v.at[0, pl.ds(0, 3), :, pl.ds(0, 256)])
    weight_wait(w_send, 1, w_v.at[:, pl.ds(0, 3), :, pl.ds(0, 256)])
    weight_wait(w_send, 2, w_v.at[:, :, :, pl.ds(0, 512)])
    weight_wait(w_send, 3, w_v.at[:, :, :, pl.ds(0, 256)])
    weight_wait(w_send, 4, w_v.at[:, :, :, pl.ds(0, 1024)])


def on_device(tokens, gate, filter_spectrum, skip_gain, kept_blocks, out_weight):
    constants = [jnp.asarray(t) for t in tables()]
    filt = jnp.transpose(filter_spectrum, (0, 1, 3, 2))
    hbm = pl.BlockSpec(memory_space=pl.ANY)
    vmem = pl.BlockSpec(memory_space=pltpu.VMEM)
    smem = pl.BlockSpec(memory_space=pltpu.SMEM)
    like = lambda t: pltpu.VMEM(t.shape, t.dtype)
    dma = pltpu.SemaphoreType.DMA
    blocks, twist, edge, first, last, pack, moves, mirror = constants
    return pl.pallas_call(
        kernel,
        out_shape=pltpu.VMEM((TOKENS, FEATS), BF16),
        in_specs=[hbm, hbm, hbm, smem, vmem, hbm] + [hbm] * 8,
        out_specs=vmem,
        scratch_shapes=[
            like(tokens), pltpu.VMEM((2, WIDTH, KEPT, BLOCK), F32), like(blocks), like(twist), like(edge), like(first), like(last), like(pack),
            like(moves), like(mirror),
            pltpu.VMEM((4096, 128), BF16),
            pltpu.VMEM((4096, 128), BF16),
            pltpu.VMEM((WIDTH, 256, TOKENS), BF16),
            pltpu.VMEM((2, 2 * KEPT, BLOCKS), BF16),
            pltpu.VMEM((2, WIDTH, BLOCK, KEPT), F32),
            pltpu.VMEM((8, BLOCKS), F32),
            pltpu.VMEM((2, 528, BLOCKS), BF16),
            pltpu.VMEM((528, 2 * KEPT), F32),
            pltpu.VMEM((2, 528, 2 * KEPT), BF16),
            pltpu.VMEM((528, BLOCKS), F32),
            pltpu.VMEM((2, 256, TOKENS), BF16),
            pltpu.VMEM((WIDTH, 256, TOKENS), BF16),
            pltpu.VMEM((4096, 128), BF16),
            pltpu.VMEM((2048, 128), BF16),
            pltpu.VMEM((2048, 128), BF16),
            pltpu.VMEM((32, 16 * TOKENS), BF16),
            pltpu.VMEM((16, 32, TOKENS), BF16),
            pltpu.VMEM((16, 32, TOKENS), BF16),
            pltpu.VMEM((16, 64, TOKENS), BF16),
            pltpu.VMEM((4, 4, 64, FEATS), BF16),
            dma((18,)), dma((2,)), dma, dma, dma, dma, dma((5,)), dma((5,)), dma, dma, dma, dma, dma, dma,
        ],
        compiler_params=pltpu.CompilerParams(
            collective_id=0, has_side_effects=True, vmem_limit_bytes=56 * 1024 * 1024
        ),
    )(tokens, gate.T, filt, skip_gain, kept_blocks.reshape(1, KEPT), out_weight, *constants)


def solution(mesh):
    return jax.shard_map(
        on_device,
        mesh=mesh,
        in_specs=(
            P(("row", "col"), None),
            P("row", "col"),
            P(None, None, None, ("col", "row")),
            P(("col", "row")),
            P(),
            P("col", None),
        ),
        out_specs=P(("row", "col"), None),
        check_vma=False,
    )
```

```python
import jax
import jax.numpy as jnp
import numpy as np
from jax import lax
from jax.experimental import pallas as pl
from jax.experimental.pallas import tpu as pltpu
from jax.sharding import PartitionSpec as P

SEQ = 131072
BLOCK = 128
BLOCKS = 1024
KEPT = 256
DEVICES = 256
TOKENS = SEQ // DEVICES
PAIRS = BLOCK // 2
WIDTH = 4
CHUNKS = 4
TILE = 16
FEATS = 2048
MESH = pl.DeviceIdType.MESH
BF16, F32 = jnp.bfloat16, jnp.float32


def split(table):
    high = table.astype(BF16)
    low = (table - high.astype(np.float64)).astype(BF16)
    return np.stack([high, low])


def tables():
    grid = np.arange(BLOCKS)
    angle = 2.0 * np.pi * (np.outer(2 * grid + 1, grid) % (2 * BLOCKS)) / (2 * BLOCKS)
    blocks = np.concatenate([split(np.cos(angle)), split(np.sin(angle))])
    pairs = np.arange(PAIRS)
    angle = 2.0 * np.pi * np.outer(pairs, grid) / SEQ
    cos, sin = np.cos(angle), np.sin(angle)
    masked = cos.copy()
    masked[0] = 0.0
    twist = np.stack([cos, sin, masked]).astype(np.float32)
    angle = 2.0 * np.pi * PAIRS * grid / SEQ
    edge = np.stack([np.cos(angle), np.sin(angle)]).astype(np.float32)
    j = np.arange(BLOCK)
    sign = (-1.0) ** j
    angle = 2.0 * np.pi * (np.outer(pairs, j) % BLOCK) / BLOCK
    real, imag = sign * np.cos(angle), -sign * np.sin(angle)
    imag[0] = 1.0
    first = np.zeros((2, 2, PAIRS, BLOCK, 2))
    for p in range(2):
        first[p, 0, :, :, p], first[p, 1, :, :, p] = real, imag
    first = first.reshape(256, 256)
    last = split(first.T.copy())
    last = np.concatenate([last[0], last[1], last[0]], axis=1)
    first = split(first)
    pack = np.zeros((32, WIDTH, CHUNKS, CHUNKS, 32, WIDTH), np.float32)
    for o in range(32):
        for c in range(WIDTH):
            for h in range(CHUNKS):
                pack[o, c, h, h, o, c] = 1.0
    pack = pack.reshape(512, 512).astype(BF16)
    rows = np.arange(256).reshape(16, WIDTH, CHUNKS)
    eye = np.eye(256, dtype=np.float32)
    fold = eye[rows.transpose(1, 2, 0).reshape(-1)]
    rows = rows.reshape(2, 8, WIDTH, CHUNKS)
    order = eye[rows.transpose(0, 3, 1, 2).reshape(-1)]
    moves = np.stack([fold, fold.T, order]).astype(BF16)
    offsets = np.concatenate([64 + pairs, [0], 64 - pairs[1:]])
    mirror = np.eye(BLOCK, dtype=np.float32)[offsets].astype(BF16)
    return blocks, twist, edge, first, last, pack, moves, mirror


def dot(a, b):
    return lax.dot_general(a, b, (((1,), (0,)), ((), ())), preferred_element_type=F32)


def dot_nt(a, b):
    return lax.dot_general(a, b, (((1,), (1,)), ((), ())), preferred_element_type=F32)


def dot_tn(a, b):
    return lax.dot_general(a, b, (((0,), (0,)), ((), ())), preferred_element_type=F32)


def store3(ref, rows, start, width, step, value):
    high, low = halves(value)
    ref[rows, start : start + width] = high
    ref[rows, start + step : start + step + width] = low
    ref[rows, start + 2 * step : start + 2 * step + width] = high


def halves(value):
    high = value.astype(BF16)
    return high, (value - high.astype(F32)).astype(BF16)


def kept_table(kept, blocks):
    row = lax.broadcasted_iota(jnp.int32, (KEPT, KEPT), 0)
    lane = lax.broadcasted_iota(jnp.int32, (KEPT, KEPT), 1)
    column = jnp.sum(jnp.where(row == lane, kept.astype(F32), 0.0), axis=1, keepdims=True)
    lane = lax.broadcasted_iota(jnp.int32, (KEPT, BLOCKS), 1).astype(F32)
    pick = jnp.where(lane == column, 1.0, 0.0).astype(BF16)
    return [dot(pick, blocks[i]).astype(BF16) for i in range(4)]


def prepare(kept, blocks_v, filt_v, mirror_v, tab, turned, filt_p):
    cos_high, cos_low, sin_high, sin_low = kept_table(kept[...], blocks_v)
    for i, part in enumerate([cos_high, sin_high, cos_high, sin_high, cos_low, sin_low]):
        tab[i * KEPT : i * KEPT + KEPT, :] = part
    for i, parts in enumerate([(cos_high, sin_high), (cos_high, sin_high), (cos_low, sin_low)]):
        for j in range(2):
            turned[i * BLOCKS : i * BLOCKS + BLOCKS, j * KEPT : j * KEPT + KEPT] = parts[j].T
    for i in range(2):
        for c in range(WIDTH):
            high, low = halves(filt_v[i, c])
            filt_p[i, c] = dot_nt(mirror_v[...], high) + dot_nt(mirror_v[...], low)


def convolve(z, first_v, last_v, twist_v, edge_v, tab, turned, filt_p, skip, ends, turn, spec, resp, wave, back, conv):
    for c in range(WIDTH):
        signal = z[c]
        spread = dot(first_v[0], signal) + dot(first_v[1], signal)
        rows = pl.ds(c * 128, 128)
        for p in range(2):
            at = pl.ds(p * TOKENS, TOKENS)
            re, im = spread[p * 128 : p * 128 + 64], spread[p * 128 + 64 : p * 128 + 128]
            cos, sin, masked = twist_v[0, :, at], twist_v[1, :, at], twist_v[2, :, at]
            both = jnp.concatenate([re * cos + im * sin, im * masked - re * sin], axis=0)
            store3(turn, rows, p * TOKENS, TOKENS, BLOCKS, both)
            ends[pl.ds(c, 1), at] = im[0:1]

    edge = ends[0:4, :]
    both = [edge * edge_v[0:1, :], edge * -edge_v[1:2, :], jnp.zeros((8, BLOCKS), F32)]
    store3(turn, pl.ds(512, 16), 0, BLOCKS, BLOCKS, jnp.concatenate(both, axis=0))

    spec[...] = dot(turn[...], turned[...])

    top = lax.broadcasted_iota(jnp.int32, (PAIRS, KEPT), 0) == 0
    ends_re, ends_im = [], []
    for c in range(WIDTH):
        at = c * 128
        cos_re, sin_re = spec[at : at + 64, :KEPT], spec[at : at + 64, KEPT:]
        cos_im, sin_im = spec[at + 64 : at + 128, :KEPT], spec[at + 64 : at + 128, KEPT:]
        up_re, up_im = cos_re + sin_im, cos_im - sin_re
        edge_re = spec[512 + c : 513 + c, :KEPT] - spec[516 + c : 517 + c, KEPT:]
        edge_im = -spec[516 + c : 517 + c, :KEPT] - spec[512 + c : 513 + c, KEPT:]
        down_re = jnp.where(top, edge_re, cos_re - sin_im)
        down_im = jnp.where(top, edge_im, -cos_im - sin_re)
        filt_re, filt_im = filt_p[0, c, 0:64], filt_p[1, c, 0:64]
        up_re, up_im = filt_re * up_re - filt_im * up_im, filt_re * up_im + filt_im * up_re
        filt_re, filt_im = filt_p[0, c, 64:128], filt_p[1, c, 64:128]
        down_re, down_im = filt_re * down_re - filt_im * down_im, filt_re * down_im + filt_im * down_re
        ends_re.append(jnp.concatenate([down_re[0:1], -down_im[0:1]], axis=1))
        ends_im.append(jnp.concatenate([-down_im[0:1], -down_re[0:1]], axis=1))
        down_re, down_im = jnp.where(top, 0.0, down_re), jnp.where(top, 0.0, down_im)
        both = jnp.concatenate(
            [
                jnp.concatenate([up_re + down_re, -(up_im + down_im)], axis=1),
                jnp.concatenate([up_im - down_im, up_re - down_re], axis=1),
            ],
            axis=0,
        )
        store3(resp, pl.ds(at, 128), 0, 2 * KEPT, 2 * KEPT, both)
    both = jnp.concatenate(ends_re + ends_im + [jnp.zeros((8, 2 * KEPT), F32)], axis=0)
    store3(resp, pl.ds(512, 16), 0, 2 * KEPT, 2 * KEPT, both)

    wave[...] = dot(resp[...], tab[...])
    edge = wave[512:516, :] * edge_v[0:1, :] - wave[516:520, :] * edge_v[1:2, :]
    ends[0:4, :] = edge

    for c in range(WIDTH):
        top = lax.broadcasted_iota(jnp.int32, (PAIRS, TOKENS), 0) == 0
        start = c * 128
        for p in range(2):
            at = pl.ds(p * TOKENS, TOKENS)
            re, im = wave[pl.ds(start, 64), at], wave[pl.ds(start + 64, 64), at]
            cos, sin = twist_v[0, :, at], twist_v[1, :, at]
            low = jnp.where(top, ends[pl.ds(c, 1), at], im * cos + re * sin)
            both = jnp.concatenate([re * cos - im * sin, low], axis=0)
            high, low = halves(both)
            for i, part in enumerate([high, high, low]):
                back[c, i * 256 + p * 128 : i * 256 + p * 128 + 128, :] = part
        result = dot(last_v[...], back[c])
        conv[c] = (result * (1.0 / SEQ) + skip[c] * z[c].astype(F32)).astype(BF16)


def kernel(
    tokens, gate, filt, skip, kept, weight, blocks, twist, edge, first, last, pack, moves, mirror,
    out,
    tok_v, filt_v, blocks_v, twist_v, edge_v, first_v, last_v, pack_v, moves_v, mirror_v,
    sent, got, z, tab, turned, filt_p, ends, turn, spec, resp, wave, back, conv, packed, returned, near, near_gate, near_out,
    gate_v, gated, side, w_v,
    local, own, a_send, a_recv, g_send, g_recv, w_send, w_recv, b_send, b_recv, n_send, n_recv, m_send, m_recv,
):
    row, col = lax.axis_index("row"), lax.axis_index("col")
    zh, x, core = row // 8, lax.rem(row, 8) // 2, lax.rem(row, 2)
    low_row = lax.rem(row, 8)
    zl, y = col // 4, lax.rem(col, 4)
    as_tokens, as_channels = row * 16 + col, col * 16 + row

    same = pl.multiple_of(zh * 32, 32)
    cross = pl.multiple_of(32 - zh * 32, 32)
    loads = [
        pltpu.make_async_copy(src, dst, local.at[i])
        for i, (src, dst) in enumerate(
            [(tokens, tok_v), (pack, pack_v), (blocks, blocks_v), (moves, moves_v), (first, first_v),
             (twist, twist_v), (last, last_v), (edge, edge_v), (mirror, mirror_v),
             (gate.at[pl.ds(same, 32), :], near_gate)]
            + [(filt.at[i, :, c, :], filt_v.at[i, c]) for i in range(2) for c in range(WIDTH)]
        )
    ]
    for load in loads[:2]:
        load.start()

    barrier = pltpu.get_barrier_semaphore()

    columns_on = [lax.rem(col + i, 16) for i in range(16)]

    def greet(to_row, steps):
        for i in steps:
            pl.semaphore_signal(barrier, inc=1, device_id=(to_row, columns_on[i]), device_id_type=MESH)

    greet(row, range(1, 16))

    @pl.loop(1, 16)
    def _(s):
        greet(lax.rem(row + s, 16), range(16))

    def columns(part, width):
        return pl.ds(pl.multiple_of(core * 1024 + part * 128, 128), width)

    slices = [columns(x, 128), columns(4 + x, 128)]
    own_weight = [
        pltpu.make_async_copy(weight.at[:, at], w_v.at[zl, y, :, at], own.at[i]) for i, at in enumerate(slices)
    ]
    for load in own_weight:
        load.start()

    loads[0].wait()
    loads[1].wait()

    @pl.loop(0, 2)
    def _(part):
        wide = []
        for i in range(4):
            at = pl.ds(pl.multiple_of((part * 4 + i) * 128, 128), 128)
            wide.append(jnp.concatenate([tok_v[pl.ds(h * 128, 128), at] for h in range(CHUNKS)], axis=1))
        rows = [dot_nt(pack_v[...], jnp.concatenate(wide[i : i + 2], axis=0)).astype(BF16) for i in (0, 2)]
        for i in range(4):
            at = pl.ds(pl.multiple_of((part * 4 + i) * 512, 512), 512)
            sent[at, :] = rows[i // 2][:, i % 2 * 128 : i % 2 * 128 + 128]

    pl.semaphore_wait(barrier, DEVICES - 1)

    def tile(index):
        return pl.ds(pl.multiple_of(index * TILE, TILE), TILE)

    def weight_copy(stage, src, dst, device):
        return pltpu.make_async_remote_copy(
            src_ref=src, dst_ref=dst, send_sem=w_send.at[stage], recv_sem=w_recv.at[stage],
            device_id=device, device_id_type=MESH,
        )

    for s in range(1, 4):
        for at in slices:
            weight_copy(0, weight.at[:, at], w_v.at[zl, y, :, at], (row, lax.rem(zl + s, 4) * 4 + y)).start()

    own_tile = pltpu.make_async_copy(sent.at[tile(as_channels)], got.at[tile(as_tokens)], a_recv)
    own_tile.start()

    def send_tokens(to_row, steps):
        for i in steps:
            pltpu.make_async_remote_copy(
                src_ref=sent.at[tile(columns_on[i] * 16 + to_row)], dst_ref=got.at[tile(as_tokens)],
                send_sem=a_send, recv_sem=a_recv, device_id=(to_row, columns_on[i]), device_id_type=MESH,
            ).start()

    send_tokens(row, range(1, 16))

    @pl.loop(1, 16)
    def _(s):
        send_tokens(lax.rem(row + s, 16), range(16))

    for load in loads[2:]:
        load.start()
    def at_x(other):
        return (zh * 8 + lax.rem(other + 4, 4) * 2 + core, col)

    def at_y(other):
        return (row, zl * 4 + lax.rem(other + 4, 4))

    for load in loads[2:]:
        load.wait()
    prepare(kept, blocks_v, filt_v, mirror_v, tab, turned, filt_p)

    def weight_wait(sem, stage, ref):
        pltpu.make_async_copy(ref, ref, sem.at[stage]).wait()

    for load in own_weight:
        load.wait()
    weight_wait(w_recv, 0, w_v.at[0, pl.ds(0, 3), :, pl.ds(0, 256)])
    for s in range(1, 4):
        part = w_v.at[:, y, :, slices[0]]
        weight_copy(1, part, part, at_y(y + s)).start()
        part = w_v.at[:, y, :, slices[1]]
        weight_copy(1, part, part, at_x(x + s)).start()

    pltpu.make_async_copy(got, got, a_recv).wait()

    def gate_at(to_col):
        return gate.at[pl.ds(cross, 32), pl.ds(pl.multiple_of(to_col * TOKENS, TOKENS), TOKENS)]

    own_gate = pltpu.make_async_copy(gate_at(col), gate_v.at[col], g_recv)
    own_gate.start()

    @pl.loop(1, 16)
    def _(s):
        to_col = lax.rem(col + s, 16)
        pltpu.make_async_remote_copy(
            src_ref=gate_at(to_col), dst_ref=gate_v.at[col], send_sem=g_send, recv_sem=g_recv,
            device_id=(row, to_col), device_id_type=MESH,
        ).start()

    weight_wait(w_recv, 1, w_v.at[:, pl.ds(0, 3), :, pl.ds(0, 256)])
    for step in (1, -1):
        part = w_v.at[:, :, :, slices[0]]
        weight_copy(2, part, part, at_x(x + step)).start()
        part = w_v.at[:, y, :, columns(4, 512)]
        weight_copy(2, part, part, at_y(y + step)).start()

    def group(ref, g):
        return ref[pl.ds(pl.multiple_of(g * 256, 256), 256), :]

    def moved(which, pieces):
        rows = [dot(moves_v[which], jnp.concatenate(pieces[i : i + 2], axis=1)) for i in range(0, len(pieces), 2)]
        return [half for pair in rows for half in (pair[:, :128], pair[:, 128:])]

    @pl.loop(0, 4)
    def _(part):
        rows = moved(0, [group(got, part * 4 + i) for i in range(4)])
        for i in range(4):
            piece = rows[i].astype(BF16)
            for c in range(WIDTH):
                for h in range(CHUNKS):
                    at = (c * 4 + h) * 16
                    z[c, tile(part * 4 + i), pl.ds(h * 128, 128)] = piece[at : at + 16, :]

    convolve(z, first_v, last_v, twist_v, edge_v, tab, turned, filt_p, skip, ends, turn, spec, resp, wave, back, conv)

    @pl.loop(0, 4)
    def _(part):
        pieces = []
        for i in range(4):
            at = tile(part * 4 + i)
            rows = [conv[c, at, pl.ds(h * 128, 128)] for c in range(WIDTH) for h in range(CHUNKS)]
            pieces.append(jnp.concatenate(rows, axis=0))
        rows = moved(1, pieces)
        for i in range(4):
            packed[pl.ds(pl.multiple_of((part * 4 + i) * 256, 256), 256), :] = rows[i].astype(BF16)

    def row_tiles(index):
        return pl.ds(pl.multiple_of(index * 256, 256), 256)

    own_near = pltpu.make_async_copy(packed.at[row_tiles(row)], near.at[row_tiles(low_row)], n_recv)
    own_near.start()

    @pl.loop(1, 8)
    def _(s):
        to_row = zh * 8 + lax.rem(low_row + s, 8)
        pltpu.make_async_remote_copy(
            src_ref=packed.at[row_tiles(to_row)], dst_ref=near.at[row_tiles(low_row)],
            send_sem=n_send, recv_sem=n_recv, device_id=(to_row, col), device_id_type=MESH,
        ).start()

    @pl.loop(0, 8)
    def _(s):
        to_row = (1 - zh) * 8 + lax.rem(low_row + s, 8)
        for to_col in columns_on:
            pltpu.make_async_remote_copy(
                src_ref=packed.at[tile(to_row * 16 + to_col)], dst_ref=returned.at[tile(col * 8 + low_row)],
                send_sem=b_send, recv_sem=b_recv, device_id=(to_row, to_col), device_id_type=MESH,
            ).start()

    weight_wait(w_recv, 2, w_v.at[:, :, :, pl.ds(0, 512)])
    for step, rows in ((1, pl.ds(0, 2)), (-1, pl.ds(2, 2))):
        part = w_v.at[rows, :, :, columns(lax.rem(x - step + 4, 4), 128)]
        weight_copy(3, part, part, at_x(x + step)).start()
        part = w_v.at[rows, lax.rem(y - step + 4, 4), :, columns(4, 512)]
        weight_copy(3, part, part, at_y(y + step)).start()

    pltpu.make_async_copy(near, near, n_recv).wait()

    @pl.loop(0, 2)
    def _(part):
        pieces = []
        for n in range(4):
            at = part * 8 + n * 2
            rows = [near[tile(s * 16 + at + i), :] for i in range(2) for s in range(8)]
            pieces.append(jnp.concatenate(rows, axis=0))
        rows = moved(2, pieces)
        for n in range(8):
            for h in range(CHUNKS):
                at = pl.ds(pl.multiple_of((part * 8 + n) * TOKENS + h * 128, 128), 128)
                from_row = n % 2 * 128 + h * 32
                piece = rows[n // 2][from_row : from_row + 32] * near_gate[:, at].astype(F32)
                near_out[part * 8 + n, :, pl.ds(h * 128, 128)] = piece.astype(BF16)

    mine = gated.at[col, pl.ds(same, 32), :]
    own_out = pltpu.make_async_copy(near_out.at[col], mine, m_recv)
    own_out.start()

    @pl.loop(1, 16)
    def _(s):
        to_col = lax.rem(col + s, 16)
        pltpu.make_async_remote_copy(
            src_ref=near_out.at[to_col], dst_ref=mine, send_sem=m_send, recv_sem=m_recv,
            device_id=(row, to_col), device_id_type=MESH,
        ).start()

    weight_wait(w_recv, 3, w_v.at[:, :, :, pl.ds(0, 256)])
    half = w_v.at[:, :, :, columns(0, 1024)]
    weight_copy(4, half, half, (row + 1 - 2 * core, col)).start()

    pltpu.make_async_copy(gate_v, gate_v, g_recv).wait()
    pltpu.make_async_copy(returned, returned, b_recv).wait()

    @pl.loop(0, 2)
    def _(part):
        rows = moved(2, [group(returned, part * 4 + i) for i in range(4)])
        for n in range(8):
            for h in range(CHUNKS):
                at = pl.ds(h * 128, 128)
                from_row = n % 2 * 128 + h * 32
                piece = rows[n // 2][from_row : from_row + 32] * gate_v[part * 8 + n, :, at].astype(F32)
                gated[part * 8 + n, pl.ds(cross, 32), at] = piece.astype(BF16)

    weight_wait(w_recv, 4, w_v.at[:, :, :, pl.ds(0, 1024)])
    pltpu.make_async_copy(near_out, near_out, m_recv).wait()

    side[...] = gated[...].reshape(1024, TOKENS).T

    @pl.loop(0, 4)
    def _(n):
        at = pl.ds(pl.multiple_of(n * 512, 512), 512)
        out[:, at] = dot(side[...], w_v[:, :, :, at].reshape(1024, 512)).astype(BF16)

    pltpu.make_async_copy(sent.at[pl.ds(0, 4080)], sent.at[pl.ds(0, 4080)], a_send).wait()
    pltpu.make_async_copy(returned, returned, b_send).wait()
    pltpu.make_async_copy(gate_v.at[pl.ds(0, 15)], gate_v.at[pl.ds(0, 15)], g_send).wait()
    pltpu.make_async_copy(near.at[pl.ds(0, 1792)], near.at[pl.ds(0, 1792)], n_send).wait()
    pltpu.make_async_copy(near_out.at[pl.ds(0, 15)], near_out.at[pl.ds(0, 15)], m_send).wait()
    weight_wait(w_send, 0, w_v.at[0, pl.ds(0, 3), :, pl.ds(0, 256)])
    weight_wait(w_send, 1, w_v.at[:, pl.ds(0, 3), :, pl.ds(0, 256)])
    weight_wait(w_send, 2, w_v.at[:, :, :, pl.ds(0, 512)])
    weight_wait(w_send, 3, w_v.at[:, :, :, pl.ds(0, 256)])
    weight_wait(w_send, 4, w_v.at[:, :, :, pl.ds(0, 1024)])


def on_device(tokens, gate, filter_spectrum, skip_gain, kept_blocks, out_weight):
    constants = [jnp.asarray(t) for t in tables()]
    filt = jnp.transpose(filter_spectrum, (0, 1, 3, 2))
    hbm = pl.BlockSpec(memory_space=pl.ANY)
    vmem = pl.BlockSpec(memory_space=pltpu.VMEM)
    smem = pl.BlockSpec(memory_space=pltpu.SMEM)
    like = lambda t: pltpu.VMEM(t.shape, t.dtype)
    dma = pltpu.SemaphoreType.DMA
    blocks, twist, edge, first, last, pack, moves, mirror = constants
    return pl.pallas_call(
        kernel,
        out_shape=pltpu.VMEM((TOKENS, FEATS), BF16),
        in_specs=[hbm, hbm, hbm, smem, vmem, hbm] + [hbm] * 8,
        out_specs=vmem,
        scratch_shapes=[
            like(tokens), pltpu.VMEM((2, WIDTH, KEPT, BLOCK), F32), like(blocks), like(twist), like(edge), like(first), like(last), like(pack),
            like(moves), like(mirror),
            pltpu.VMEM((4096, 128), BF16),
            pltpu.VMEM((4096, 128), BF16),
            pltpu.VMEM((WIDTH, 256, TOKENS), BF16),
            pltpu.VMEM((6 * KEPT, BLOCKS), BF16),
            pltpu.VMEM((3 * BLOCKS, 2 * KEPT), BF16),
            pltpu.VMEM((2, WIDTH, BLOCK, KEPT), F32),
            pltpu.VMEM((8, BLOCKS), F32),
            pltpu.VMEM((528, 3 * BLOCKS), BF16),
            pltpu.VMEM((528, 2 * KEPT), F32),
            pltpu.VMEM((528, 6 * KEPT), BF16),
            pltpu.VMEM((528, BLOCKS), F32),
            pltpu.VMEM((WIDTH, 768, TOKENS), BF16),
            pltpu.VMEM((WIDTH, 256, TOKENS), BF16),
            pltpu.VMEM((4096, 128), BF16),
            pltpu.VMEM((2048, 128), BF16),
            pltpu.VMEM((2048, 128), BF16),
            pltpu.VMEM((32, 16 * TOKENS), BF16),
            pltpu.VMEM((16, 32, TOKENS), BF16),
            pltpu.VMEM((16, 32, TOKENS), BF16),
            pltpu.VMEM((16, 64, TOKENS), BF16),
            pltpu.VMEM((TOKENS, 1024), BF16),
            pltpu.VMEM((4, 4, 64, FEATS), BF16),
            dma((18,)), dma((2,)), dma, dma, dma, dma, dma((5,)), dma((5,)), dma, dma, dma, dma, dma, dma,
        ],
        compiler_params=pltpu.CompilerParams(
            collective_id=0, has_side_effects=True, vmem_limit_bytes=56 * 1024 * 1024
        ),
    )(tokens, gate.T, filt, skip_gain, kept_blocks.reshape(1, KEPT), out_weight, *constants)


def solution(mesh):
    return jax.shard_map(
        on_device,
        mesh=mesh,
        in_specs=(
            P(("row", "col"), None),
            P("row", "col"),
            P(None, None, None, ("col", "row")),
            P(("col", "row")),
            P(),
            P("col", None),
        ),
        out_specs=P(("row", "col"), None),
        check_vma=False,
    )
```

```python
import jax
import jax.numpy as jnp
import numpy as np
from jax import lax
from jax.experimental import pallas as pl
from jax.experimental.pallas import tpu as pltpu
from jax.sharding import PartitionSpec as P

SEQ = 131072
BLOCK = 128
BLOCKS = 1024
KEPT = 256
DEVICES = 256
TOKENS = SEQ // DEVICES
PAIRS = BLOCK // 2
WIDTH = 4
CHUNKS = 4
TILE = 16
FEATS = 2048
MESH = pl.DeviceIdType.MESH
BF16, F32 = jnp.bfloat16, jnp.float32


def split(table):
    high = table.astype(BF16)
    low = (table - high.astype(np.float64)).astype(BF16)
    return np.stack([high, low])


def tables():
    grid = np.arange(BLOCKS)
    angle = 2.0 * np.pi * (np.outer(2 * grid + 1, grid) % (2 * BLOCKS)) / (2 * BLOCKS)
    blocks = np.concatenate([split(np.cos(angle)), split(np.sin(angle))])
    pairs = np.arange(PAIRS)
    angle = 2.0 * np.pi * np.outer(pairs, grid) / SEQ
    cos, sin = np.cos(angle), np.sin(angle)
    masked = cos.copy()
    masked[0] = 0.0
    twist = np.stack([cos, sin, masked]).astype(np.float32)
    angle = 2.0 * np.pi * PAIRS * grid / SEQ
    edge = np.stack([np.cos(angle), np.sin(angle)]).astype(np.float32)
    j = np.arange(BLOCK)
    sign = (-1.0) ** j
    angle = 2.0 * np.pi * (np.outer(pairs, j) % BLOCK) / BLOCK
    real, imag = sign * np.cos(angle), -sign * np.sin(angle)
    imag[0] = 1.0
    first = np.zeros((2, 2, PAIRS, BLOCK, 2))
    for p in range(2):
        first[p, 0, :, :, p], first[p, 1, :, :, p] = real, imag
    first = first.reshape(256, 256)
    last = split(first.T.copy())
    last = np.concatenate([last[0], last[1], last[0]], axis=1)
    first = split(first)
    pack = np.zeros((32, WIDTH, CHUNKS, CHUNKS, 32, WIDTH), np.float32)
    for o in range(32):
        for c in range(WIDTH):
            for h in range(CHUNKS):
                pack[o, c, h, h, o, c] = 1.0
    pack = pack.reshape(512, 512).astype(BF16)
    rows = np.arange(256).reshape(16, WIDTH, CHUNKS)
    eye = np.eye(256, dtype=np.float32)
    fold = eye[rows.transpose(1, 2, 0).reshape(-1)]
    rows = rows.reshape(2, 8, WIDTH, CHUNKS)
    order = eye[rows.transpose(0, 3, 1, 2).reshape(-1)]
    moves = np.stack([fold, fold.T, order]).astype(BF16)
    offsets = np.concatenate([64 + pairs, [0], 64 - pairs[1:]])
    mirror = np.eye(BLOCK, dtype=np.float32)[offsets].astype(BF16)
    return blocks, twist, edge, first, last, pack, moves, mirror


def dot(a, b):
    return lax.dot_general(a, b, (((1,), (0,)), ((), ())), preferred_element_type=F32)


def dot_nt(a, b):
    return lax.dot_general(a, b, (((1,), (1,)), ((), ())), preferred_element_type=F32)


def dot_tn(a, b):
    return lax.dot_general(a, b, (((0,), (0,)), ((), ())), preferred_element_type=F32)


def store3(ref, rows, start, width, step, value):
    high, low = halves(value)
    ref[rows, start : start + width] = high
    ref[rows, start + step : start + step + width] = low
    ref[rows, start + 2 * step : start + 2 * step + width] = high


def halves(value):
    high = value.astype(BF16)
    return high, (value - high.astype(F32)).astype(BF16)


def kept_table(kept, blocks):
    row = lax.broadcasted_iota(jnp.int32, (KEPT, KEPT), 0)
    lane = lax.broadcasted_iota(jnp.int32, (KEPT, KEPT), 1)
    column = jnp.sum(jnp.where(row == lane, kept.astype(F32), 0.0), axis=1, keepdims=True)
    lane = lax.broadcasted_iota(jnp.int32, (KEPT, BLOCKS), 1).astype(F32)
    pick = jnp.where(lane == column, 1.0, 0.0).astype(BF16)
    return [dot(pick, blocks[i]).astype(BF16) for i in range(4)]


def prepare(kept, blocks_v, filt_v, mirror_v, tab, turned, filt_p):
    cos_high, cos_low, sin_high, sin_low = kept_table(kept[...], blocks_v)
    for i, part in enumerate([cos_high, sin_high, cos_high, sin_high, cos_low, sin_low]):
        tab[i * KEPT : i * KEPT + KEPT, :] = part
    for i, parts in enumerate([(cos_high, sin_high), (cos_high, sin_high), (cos_low, sin_low)]):
        for j in range(2):
            turned[i * BLOCKS : i * BLOCKS + BLOCKS, j * KEPT : j * KEPT + KEPT] = parts[j].T
    for i in range(2):
        for c in range(WIDTH):
            high, low = halves(filt_v[i, c])
            filt_p[i, c] = dot_nt(mirror_v[...], high) + dot_nt(mirror_v[...], low)


def convolve(z, first_v, last_v, twist_v, edge_v, tab, turned, filt_p, skip, ends, turn, spec, resp, wave, back, conv):
    for c in range(WIDTH):
        signal = z[c]
        spread = dot(first_v[0], signal) + dot(first_v[1], signal)
        rows = pl.ds(c * 128, 128)
        for p in range(2):
            at = pl.ds(p * TOKENS, TOKENS)
            re, im = spread[p * 128 : p * 128 + 64], spread[p * 128 + 64 : p * 128 + 128]
            cos, sin, masked = twist_v[0, :, at], twist_v[1, :, at], twist_v[2, :, at]
            both = jnp.concatenate([re * cos + im * sin, im * masked - re * sin], axis=0)
            store3(turn, rows, p * TOKENS, TOKENS, BLOCKS, both)
            ends[pl.ds(c, 1), at] = im[0:1]

    edge = ends[0:4, :]
    both = [edge * edge_v[0:1, :], edge * -edge_v[1:2, :], jnp.zeros((8, BLOCKS), F32)]
    store3(turn, pl.ds(512, 16), 0, BLOCKS, BLOCKS, jnp.concatenate(both, axis=0))

    spec[...] = dot(turn[...], turned[...])

    top = lax.broadcasted_iota(jnp.int32, (PAIRS, KEPT), 0) == 0
    ends_re, ends_im = [], []
    for c in range(WIDTH):
        at = c * 128
        cos_re, sin_re = spec[at : at + 64, :KEPT], spec[at : at + 64, KEPT:]
        cos_im, sin_im = spec[at + 64 : at + 128, :KEPT], spec[at + 64 : at + 128, KEPT:]
        up_re, up_im = cos_re + sin_im, cos_im - sin_re
        edge_re = spec[512 + c : 513 + c, :KEPT] - spec[516 + c : 517 + c, KEPT:]
        edge_im = -spec[516 + c : 517 + c, :KEPT] - spec[512 + c : 513 + c, KEPT:]
        down_re = jnp.where(top, edge_re, cos_re - sin_im)
        down_im = jnp.where(top, edge_im, -cos_im - sin_re)
        filt_re, filt_im = filt_p[0, c, 0:64], filt_p[1, c, 0:64]
        up_re, up_im = filt_re * up_re - filt_im * up_im, filt_re * up_im + filt_im * up_re
        filt_re, filt_im = filt_p[0, c, 64:128], filt_p[1, c, 64:128]
        down_re, down_im = filt_re * down_re - filt_im * down_im, filt_re * down_im + filt_im * down_re
        ends_re.append(jnp.concatenate([down_re[0:1], -down_im[0:1]], axis=1))
        ends_im.append(jnp.concatenate([-down_im[0:1], -down_re[0:1]], axis=1))
        down_re, down_im = jnp.where(top, 0.0, down_re), jnp.where(top, 0.0, down_im)
        both = jnp.concatenate(
            [
                jnp.concatenate([up_re + down_re, -(up_im + down_im)], axis=1),
                jnp.concatenate([up_im - down_im, up_re - down_re], axis=1),
            ],
            axis=0,
        )
        store3(resp, pl.ds(at, 128), 0, 2 * KEPT, 2 * KEPT, both)
    both = jnp.concatenate(ends_re + ends_im + [jnp.zeros((8, 2 * KEPT), F32)], axis=0)
    store3(resp, pl.ds(512, 16), 0, 2 * KEPT, 2 * KEPT, both)

    wave[...] = dot(resp[...], tab[...])
    edge = wave[512:516, :] * edge_v[0:1, :] - wave[516:520, :] * edge_v[1:2, :]
    ends[0:4, :] = edge

    for c in range(WIDTH):
        top = lax.broadcasted_iota(jnp.int32, (PAIRS, TOKENS), 0) == 0
        start = c * 128
        for p in range(2):
            at = pl.ds(p * TOKENS, TOKENS)
            re, im = wave[pl.ds(start, 64), at], wave[pl.ds(start + 64, 64), at]
            cos, sin = twist_v[0, :, at], twist_v[1, :, at]
            low = jnp.where(top, ends[pl.ds(c, 1), at], im * cos + re * sin)
            both = jnp.concatenate([re * cos - im * sin, low], axis=0)
            high, low = halves(both)
            for i, part in enumerate([high, high, low]):
                back[c, i * 256 + p * 128 : i * 256 + p * 128 + 128, :] = part
        result = dot(last_v[...], back[c])
        conv[c] = (result * (1.0 / SEQ) + skip[c] * z[c].astype(F32)).astype(BF16)


def kernel(
    tokens, gate, filt, skip, kept, weight, blocks, twist, edge, first, last, pack, moves, mirror,
    out,
    tok_v, filt_v, blocks_v, twist_v, edge_v, first_v, last_v, pack_v, moves_v, mirror_v,
    sent, got, z, tab, turned, filt_p, ends, turn, spec, resp, wave, back, conv, packed, returned, near, near_gate, near_out,
    gate_v, gated_near, gated_far, side, total, w_v,
    local, own, a_send, a_recv, g_send, g_recv, w_send, w_recv, b_send, b_recv, n_send, n_recv, m_send, m_recv,
):
    row, col = lax.axis_index("row"), lax.axis_index("col")
    zh, x, core = row // 8, lax.rem(row, 8) // 2, lax.rem(row, 2)
    low_row = lax.rem(row, 8)
    zl, y = col // 4, lax.rem(col, 4)
    as_tokens, as_channels = row * 16 + col, col * 16 + row

    same = pl.multiple_of(zh * 32, 32)
    cross = pl.multiple_of(32 - zh * 32, 32)
    loads = [
        pltpu.make_async_copy(src, dst, local.at[i])
        for i, (src, dst) in enumerate(
            [(tokens, tok_v), (pack, pack_v), (blocks, blocks_v), (moves, moves_v), (first, first_v),
             (twist, twist_v), (last, last_v), (edge, edge_v), (mirror, mirror_v),
             (gate.at[pl.ds(same, 32), :], near_gate)]
            + [(filt.at[i, :, c, :], filt_v.at[i, c]) for i in range(2) for c in range(WIDTH)]
        )
    ]
    for load in loads[:2]:
        load.start()

    barrier = pltpu.get_barrier_semaphore()

    columns_on = [lax.rem(col + i, 16) for i in range(16)]

    def greet(to_row, steps):
        for i in steps:
            pl.semaphore_signal(barrier, inc=1, device_id=(to_row, columns_on[i]), device_id_type=MESH)

    greet(row, range(1, 16))

    @pl.loop(1, 16)
    def _(s):
        greet(lax.rem(row + s, 16), range(16))

    def columns(part, width):
        return pl.ds(pl.multiple_of(core * 1024 + part * 128, 128), width)

    slices = [columns(x, 128), columns(4 + x, 128)]
    own_weight = [
        pltpu.make_async_copy(weight.at[:, at], w_v.at[zl, y, :, at], own.at[i]) for i, at in enumerate(slices)
    ]
    for load in own_weight:
        load.start()

    loads[0].wait()
    loads[1].wait()

    @pl.loop(0, 2)
    def _(part):
        wide = []
        for i in range(4):
            at = pl.ds(pl.multiple_of((part * 4 + i) * 128, 128), 128)
            wide.append(jnp.concatenate([tok_v[pl.ds(h * 128, 128), at] for h in range(CHUNKS)], axis=1))
        rows = [dot_nt(pack_v[...], jnp.concatenate(wide[i : i + 2], axis=0)).astype(BF16) for i in (0, 2)]
        for i in range(4):
            at = pl.ds(pl.multiple_of((part * 4 + i) * 512, 512), 512)
            sent[at, :] = rows[i // 2][:, i % 2 * 128 : i % 2 * 128 + 128]

    pl.semaphore_wait(barrier, DEVICES - 1)

    def tile(index):
        return pl.ds(pl.multiple_of(index * TILE, TILE), TILE)

    def weight_copy(stage, src, dst, device):
        return pltpu.make_async_remote_copy(
            src_ref=src, dst_ref=dst, send_sem=w_send.at[stage], recv_sem=w_recv.at[stage],
            device_id=device, device_id_type=MESH,
        )

    for s in range(1, 4):
        for at in slices:
            weight_copy(0, weight.at[:, at], w_v.at[zl, y, :, at], (row, lax.rem(zl + s, 4) * 4 + y)).start()

    own_tile = pltpu.make_async_copy(sent.at[tile(as_channels)], got.at[tile(as_tokens)], a_recv)
    own_tile.start()

    def send_tokens(to_row, steps):
        for i in steps:
            pltpu.make_async_remote_copy(
                src_ref=sent.at[tile(columns_on[i] * 16 + to_row)], dst_ref=got.at[tile(as_tokens)],
                send_sem=a_send, recv_sem=a_recv, device_id=(to_row, columns_on[i]), device_id_type=MESH,
            ).start()

    send_tokens(row, range(1, 16))

    @pl.loop(1, 16)
    def _(s):
        send_tokens(lax.rem(row + s, 16), range(16))

    for load in loads[2:]:
        load.start()
    def at_x(other):
        return (zh * 8 + lax.rem(other + 4, 4) * 2 + core, col)

    def at_y(other):
        return (row, zl * 4 + lax.rem(other + 4, 4))

    for load in loads[2:]:
        load.wait()
    prepare(kept, blocks_v, filt_v, mirror_v, tab, turned, filt_p)

    def weight_wait(sem, stage, ref):
        pltpu.make_async_copy(ref, ref, sem.at[stage]).wait()

    for load in own_weight:
        load.wait()
    weight_wait(w_recv, 0, w_v.at[0, pl.ds(0, 3), :, pl.ds(0, 256)])
    for s in range(1, 4):
        part = w_v.at[:, y, :, slices[0]]
        weight_copy(1, part, part, at_y(y + s)).start()
        part = w_v.at[:, y, :, slices[1]]
        weight_copy(1, part, part, at_x(x + s)).start()

    pltpu.make_async_copy(got, got, a_recv).wait()

    def far_column(s):
        ahead = lax.rem(col + s - 1 + s // 9, 8)
        return lax.rem(col // 8 + 1 + s // 9, 2) * 8 + ahead

    def gate_at(to_col):
        return gate.at[pl.ds(cross, 32), pl.ds(pl.multiple_of(to_col * TOKENS, TOKENS), TOKENS)]

    own_gate = pltpu.make_async_copy(gate_at(col), gate_v.at[col], g_recv)
    own_gate.start()

    @pl.loop(1, 16)
    def _(s):
        to_col = far_column(s)
        pltpu.make_async_remote_copy(
            src_ref=gate_at(to_col), dst_ref=gate_v.at[col], send_sem=g_send, recv_sem=g_recv,
            device_id=(row, to_col), device_id_type=MESH,
        ).start()

    weight_wait(w_recv, 1, w_v.at[:, pl.ds(0, 3), :, pl.ds(0, 256)])
    for step in (1, -1):
        part = w_v.at[:, :, :, slices[0]]
        weight_copy(2, part, part, at_x(x + step)).start()
        part = w_v.at[:, y, :, columns(4, 512)]
        weight_copy(2, part, part, at_y(y + step)).start()

    def group(ref, g):
        return ref[pl.ds(pl.multiple_of(g * 256, 256), 256), :]

    def moved(which, pieces):
        rows = [dot(moves_v[which], jnp.concatenate(pieces[i : i + 2], axis=1)) for i in range(0, len(pieces), 2)]
        return [half for pair in rows for half in (pair[:, :128], pair[:, 128:])]

    @pl.loop(0, 4)
    def _(part):
        rows = moved(0, [group(got, part * 4 + i) for i in range(4)])
        for i in range(4):
            piece = rows[i].astype(BF16)
            for c in range(WIDTH):
                for h in range(CHUNKS):
                    at = (c * 4 + h) * 16
                    z[c, tile(part * 4 + i), pl.ds(h * 128, 128)] = piece[at : at + 16, :]

    convolve(z, first_v, last_v, twist_v, edge_v, tab, turned, filt_p, skip, ends, turn, spec, resp, wave, back, conv)

    @pl.loop(0, 4)
    def _(part):
        pieces = []
        for i in range(4):
            at = tile(part * 4 + i)
            rows = [conv[c, at, pl.ds(h * 128, 128)] for c in range(WIDTH) for h in range(CHUNKS)]
            pieces.append(jnp.concatenate(rows, axis=0))
        rows = moved(1, pieces)
        for i in range(4):
            packed[pl.ds(pl.multiple_of((part * 4 + i) * 256, 256), 256), :] = rows[i].astype(BF16)

    def row_tiles(index):
        return pl.ds(pl.multiple_of(index * 256, 256), 256)

    own_near = pltpu.make_async_copy(packed.at[row_tiles(row)], near.at[row_tiles(low_row)], n_recv)
    own_near.start()

    def send_near():
        @pl.loop(1, 8)
        def _(s):
            to_row = zh * 8 + lax.rem(low_row + s, 8)
            pltpu.make_async_remote_copy(
                src_ref=packed.at[row_tiles(to_row)], dst_ref=near.at[row_tiles(low_row)],
                send_sem=n_send, recv_sem=n_recv, device_id=(to_row, col), device_id_type=MESH,
            ).start()

    pl.when(zh == 0)(send_near)

    @pl.loop(0, 3)
    def _(s):
        to_row = (1 - zh) * 8 + lax.rem(low_row + s, 8)
        for to_col in columns_on:
            pltpu.make_async_remote_copy(
                src_ref=packed.at[tile(to_row * 16 + to_col)], dst_ref=returned.at[tile(col * 8 + low_row)],
                send_sem=b_send, recv_sem=b_recv, device_id=(to_row, to_col), device_id_type=MESH,
            ).start()

    pl.when(zh == 1)(send_near)

    @pl.loop(3, 8)
    def _(s):
        to_row = (1 - zh) * 8 + lax.rem(low_row + s, 8)
        for to_col in columns_on:
            pltpu.make_async_remote_copy(
                src_ref=packed.at[tile(to_row * 16 + to_col)], dst_ref=returned.at[tile(col * 8 + low_row)],
                send_sem=b_send, recv_sem=b_recv, device_id=(to_row, to_col), device_id_type=MESH,
            ).start()

    weight_wait(w_recv, 2, w_v.at[:, :, :, pl.ds(0, 512)])
    for step, rows in ((1, pl.ds(0, 2)), (-1, pl.ds(2, 2))):
        part = w_v.at[rows, :, :, columns(lax.rem(x - step + 4, 4), 128)]
        weight_copy(3, part, part, at_x(x + step)).start()
        part = w_v.at[rows, lax.rem(y - step + 4, 4), :, columns(4, 512)]
        weight_copy(3, part, part, at_y(y + step)).start()

    pltpu.make_async_copy(near, near, n_recv).wait()

    @pl.loop(0, 2)
    def _(part):
        pieces = []
        for n in range(4):
            at = part * 8 + n * 2
            rows = [near[tile(s * 16 + at + i), :] for i in range(2) for s in range(8)]
            pieces.append(jnp.concatenate(rows, axis=0))
        rows = moved(2, pieces)
        for n in range(8):
            for h in range(CHUNKS):
                at = pl.ds(pl.multiple_of((part * 8 + n) * TOKENS + h * 128, 128), 128)
                from_row = n % 2 * 128 + h * 32
                piece = rows[n // 2][from_row : from_row + 32] * near_gate[:, at].astype(F32)
                near_out[part * 8 + n, :, pl.ds(h * 128, 128)] = piece.astype(BF16)

    mine = gated_near.at[col]
    own_out = pltpu.make_async_copy(near_out.at[col], mine, m_recv)
    own_out.start()

    @pl.loop(1, 16)
    def _(s):
        to_col = far_column(s)
        pltpu.make_async_remote_copy(
            src_ref=near_out.at[to_col], dst_ref=mine, send_sem=m_send, recv_sem=m_recv,
            device_id=(row, to_col), device_id_type=MESH,
        ).start()

    weight_wait(w_recv, 3, w_v.at[:, :, :, pl.ds(0, 256)])
    half = w_v.at[:, :, :, columns(0, 1024)]
    weight_copy(4, half, half, (row + 1 - 2 * core, col)).start()

    pltpu.make_async_copy(gate_v, gate_v, g_recv).wait()
    pltpu.make_async_copy(returned, returned, b_recv).wait()

    @pl.loop(0, 2)
    def _(part):
        rows = moved(2, [group(returned, part * 4 + i) for i in range(4)])
        for n in range(8):
            for h in range(CHUNKS):
                at = pl.ds(h * 128, 128)
                from_row = n % 2 * 128 + h * 32
                piece = rows[n // 2][from_row : from_row + 32] * gate_v[part * 8 + n, :, at].astype(F32)
                gated_far[part * 8 + n, :, at] = piece.astype(BF16)

    weight_wait(w_recv, 4, w_v.at[:, :, :, pl.ds(0, 1024)])

    def project(start, at):
        return dot(side[...], w_v[:, :, pl.ds(start, 32), at].reshape(512, 512))

    side[...] = gated_far[...].reshape(512, TOKENS).T

    @pl.loop(0, 4)
    def _(n):
        at = pl.ds(pl.multiple_of(n * 512, 512), 512)
        total[:, at] = project(cross, at)

    pltpu.make_async_copy(near_out, near_out, m_recv).wait()
    side[...] = gated_near[...].reshape(512, TOKENS).T

    @pl.loop(0, 4)
    def _(n):
        at = pl.ds(pl.multiple_of(n * 512, 512), 512)
        out[:, at] = (total[:, at] + project(same, at)).astype(BF16)

    pltpu.make_async_copy(sent.at[pl.ds(0, 4080)], sent.at[pl.ds(0, 4080)], a_send).wait()
    pltpu.make_async_copy(returned, returned, b_send).wait()
    pltpu.make_async_copy(gate_v.at[pl.ds(0, 15)], gate_v.at[pl.ds(0, 15)], g_send).wait()
    pltpu.make_async_copy(near.at[pl.ds(0, 1792)], near.at[pl.ds(0, 1792)], n_send).wait()
    pltpu.make_async_copy(near_out.at[pl.ds(0, 15)], near_out.at[pl.ds(0, 15)], m_send).wait()
    weight_wait(w_send, 0, w_v.at[0, pl.ds(0, 3), :, pl.ds(0, 256)])
    weight_wait(w_send, 1, w_v.at[:, pl.ds(0, 3), :, pl.ds(0, 256)])
    weight_wait(w_send, 2, w_v.at[:, :, :, pl.ds(0, 512)])
    weight_wait(w_send, 3, w_v.at[:, :, :, pl.ds(0, 256)])
    weight_wait(w_send, 4, w_v.at[:, :, :, pl.ds(0, 1024)])


def on_device(tokens, gate, filter_spectrum, skip_gain, kept_blocks, out_weight):
    constants = [jnp.asarray(t) for t in tables()]
    filt = jnp.transpose(filter_spectrum, (0, 1, 3, 2))
    hbm = pl.BlockSpec(memory_space=pl.ANY)
    vmem = pl.BlockSpec(memory_space=pltpu.VMEM)
    smem = pl.BlockSpec(memory_space=pltpu.SMEM)
    like = lambda t: pltpu.VMEM(t.shape, t.dtype)
    dma = pltpu.SemaphoreType.DMA
    blocks, twist, edge, first, last, pack, moves, mirror = constants
    return pl.pallas_call(
        kernel,
        out_shape=pltpu.VMEM((TOKENS, FEATS), BF16),
        in_specs=[hbm, hbm, hbm, smem, vmem, hbm] + [hbm] * 8,
        out_specs=vmem,
        scratch_shapes=[
            like(tokens), pltpu.VMEM((2, WIDTH, KEPT, BLOCK), F32), like(blocks), like(twist), like(edge), like(first), like(last), like(pack),
            like(moves), like(mirror),
            pltpu.VMEM((4096, 128), BF16),
            pltpu.VMEM((4096, 128), BF16),
            pltpu.VMEM((WIDTH, 256, TOKENS), BF16),
            pltpu.VMEM((6 * KEPT, BLOCKS), BF16),
            pltpu.VMEM((3 * BLOCKS, 2 * KEPT), BF16),
            pltpu.VMEM((2, WIDTH, BLOCK, KEPT), F32),
            pltpu.VMEM((8, BLOCKS), F32),
            pltpu.VMEM((528, 3 * BLOCKS), BF16),
            pltpu.VMEM((528, 2 * KEPT), F32),
            pltpu.VMEM((528, 6 * KEPT), BF16),
            pltpu.VMEM((528, BLOCKS), F32),
            pltpu.VMEM((WIDTH, 768, TOKENS), BF16),
            pltpu.VMEM((WIDTH, 256, TOKENS), BF16),
            pltpu.VMEM((4096, 128), BF16),
            pltpu.VMEM((2048, 128), BF16),
            pltpu.VMEM((2048, 128), BF16),
            pltpu.VMEM((32, 16 * TOKENS), BF16),
            pltpu.VMEM((16, 32, TOKENS), BF16),
            pltpu.VMEM((16, 32, TOKENS), BF16),
            pltpu.VMEM((16, 32, TOKENS), BF16),
            pltpu.VMEM((16, 32, TOKENS), BF16),
            pltpu.VMEM((TOKENS, 512), BF16),
            pltpu.VMEM((TOKENS, FEATS), F32),
            pltpu.VMEM((4, 4, 64, FEATS), BF16),
            dma((18,)), dma((2,)), dma, dma, dma, dma, dma((5,)), dma((5,)), dma, dma, dma, dma, dma, dma,
        ],
        compiler_params=pltpu.CompilerParams(
            collective_id=0, has_side_effects=True, vmem_limit_bytes=56 * 1024 * 1024
        ),
    )(tokens, gate.T, filt, skip_gain, kept_blocks.reshape(1, KEPT), out_weight, *constants)


def solution(mesh):
    return jax.shard_map(
        on_device,
        mesh=mesh,
        in_specs=(
            P(("row", "col"), None),
            P("row", "col"),
            P(None, None, None, ("col", "row")),
            P(("col", "row")),
            P(),
            P("col", None),
        ),
        out_specs=P(("row", "col"), None),
        check_vma=False,
    )
```

```python
import jax
import jax.numpy as jnp
import numpy as np
from jax import lax
from jax.experimental import pallas as pl
from jax.experimental.pallas import tpu as pltpu
from jax.sharding import PartitionSpec as P

SEQ = 131072
BLOCK = 128
BLOCKS = 1024
KEPT = 256
DEVICES = 256
TOKENS = SEQ // DEVICES
PAIRS = BLOCK // 2
WIDTH = 4
CHUNKS = 4
TILE = 16
FEATS = 2048
MESH = pl.DeviceIdType.MESH
BF16, F32 = jnp.bfloat16, jnp.float32


def split(table):
    high = table.astype(BF16)
    low = (table - high.astype(np.float64)).astype(BF16)
    return np.stack([high, low])


def tables():
    grid = np.arange(BLOCKS)
    angle = 2.0 * np.pi * (np.outer(2 * grid + 1, grid) % (2 * BLOCKS)) / (2 * BLOCKS)
    blocks = np.concatenate([split(np.cos(angle)), split(np.sin(angle))])
    pairs = np.arange(PAIRS)
    angle = 2.0 * np.pi * np.outer(pairs, grid) / SEQ
    cos, sin = np.cos(angle), np.sin(angle)
    masked = cos.copy()
    masked[0] = 0.0
    twist = np.stack([cos, sin, masked]).astype(np.float32)
    angle = 2.0 * np.pi * PAIRS * grid / SEQ
    edge = np.stack([np.cos(angle), np.sin(angle)]).astype(np.float32)
    j = np.arange(BLOCK)
    sign = (-1.0) ** j
    angle = 2.0 * np.pi * (np.outer(pairs, j) % BLOCK) / BLOCK
    real, imag = sign * np.cos(angle), -sign * np.sin(angle)
    imag[0] = 1.0
    first = np.zeros((2, 2, PAIRS, BLOCK, 2))
    for p in range(2):
        first[p, 0, :, :, p], first[p, 1, :, :, p] = real, imag
    first = first.reshape(256, 256)
    last = split(first.T.copy())
    last = np.concatenate([last[0], last[1], last[0]], axis=1)
    first = split(first)
    pack = np.zeros((32, WIDTH, CHUNKS, CHUNKS, 32, WIDTH), np.float32)
    for o in range(32):
        for c in range(WIDTH):
            for h in range(CHUNKS):
                pack[o, c, h, h, o, c] = 1.0
    pack = pack.reshape(512, 512).astype(BF16)
    rows = np.arange(256).reshape(16, WIDTH, CHUNKS)
    eye = np.eye(256, dtype=np.float32)
    fold = eye[rows.transpose(1, 2, 0).reshape(-1)]
    rows = rows.reshape(2, 8, WIDTH, CHUNKS)
    order = eye[rows.transpose(0, 3, 1, 2).reshape(-1)]
    moves = np.stack([fold, fold.T, order]).astype(BF16)
    offsets = np.concatenate([64 + pairs, [0], 64 - pairs[1:]])
    mirror = np.eye(BLOCK, dtype=np.float32)[offsets].astype(BF16)
    return blocks, twist, edge, first, last, pack, moves, mirror


def dot(a, b):
    return lax.dot_general(a, b, (((1,), (0,)), ((), ())), preferred_element_type=F32)


def dot_nt(a, b):
    return lax.dot_general(a, b, (((1,), (1,)), ((), ())), preferred_element_type=F32)


def dot_tn(a, b):
    return lax.dot_general(a, b, (((0,), (0,)), ((), ())), preferred_element_type=F32)


def store3(ref, rows, start, width, step, value):
    high, low = halves(value)
    ref[rows, start : start + width] = high
    ref[rows, start + step : start + step + width] = low
    ref[rows, start + 2 * step : start + 2 * step + width] = high


def halves(value):
    high = value.astype(BF16)
    return high, (value - high.astype(F32)).astype(BF16)


def kept_table(kept, blocks):
    row = lax.broadcasted_iota(jnp.int32, (KEPT, KEPT), 0)
    lane = lax.broadcasted_iota(jnp.int32, (KEPT, KEPT), 1)
    column = jnp.sum(jnp.where(row == lane, kept.astype(F32), 0.0), axis=1, keepdims=True)
    lane = lax.broadcasted_iota(jnp.int32, (KEPT, BLOCKS), 1).astype(F32)
    pick = jnp.where(lane == column, 1.0, 0.0).astype(BF16)
    return [dot(pick, blocks[i]).astype(BF16) for i in range(4)]


def prepare(kept, blocks_v, filt_v, mirror_v, tab, turned, filt_p):
    cos_high, cos_low, sin_high, sin_low = kept_table(kept[...], blocks_v)
    for i, part in enumerate([cos_high, sin_high, cos_high, sin_high, cos_low, sin_low]):
        tab[i * KEPT : i * KEPT + KEPT, :] = part
    for i, parts in enumerate([(cos_high, sin_high), (cos_high, sin_high), (cos_low, sin_low)]):
        for j in range(2):
            turned[i * BLOCKS : i * BLOCKS + BLOCKS, j * KEPT : j * KEPT + KEPT] = parts[j].T
    for i in range(2):
        for c in range(WIDTH):
            high, low = halves(filt_v[i, c])
            filt_p[i, c] = dot_nt(mirror_v[...], high) + dot_nt(mirror_v[...], low)


def convolve(z, first_v, last_v, twist_v, edge_v, tab, turned, filt_p, skip, ends, turn, spec, resp, wave, back, conv):
    for c in range(WIDTH):
        signal = z[c]
        spread = dot(first_v[0], signal) + dot(first_v[1], signal)
        rows = pl.ds(c * 128, 128)
        for p in range(2):
            at = pl.ds(p * TOKENS, TOKENS)
            re, im = spread[p * 128 : p * 128 + 64], spread[p * 128 + 64 : p * 128 + 128]
            cos, sin, masked = twist_v[0, :, at], twist_v[1, :, at], twist_v[2, :, at]
            both = jnp.concatenate([re * cos + im * sin, im * masked - re * sin], axis=0)
            store3(turn, rows, p * TOKENS, TOKENS, BLOCKS, both)
            ends[pl.ds(c, 1), at] = im[0:1]

    edge = ends[0:4, :]
    both = [edge * edge_v[0:1, :], edge * -edge_v[1:2, :], jnp.zeros((8, BLOCKS), F32)]
    store3(turn, pl.ds(512, 16), 0, BLOCKS, BLOCKS, jnp.concatenate(both, axis=0))

    spec[...] = dot(turn[...], turned[...])

    top = lax.broadcasted_iota(jnp.int32, (PAIRS, KEPT), 0) == 0
    ends_re, ends_im = [], []
    for c in range(WIDTH):
        at = c * 128
        cos_re, sin_re = spec[at : at + 64, :KEPT], spec[at : at + 64, KEPT:]
        cos_im, sin_im = spec[at + 64 : at + 128, :KEPT], spec[at + 64 : at + 128, KEPT:]
        up_re, up_im = cos_re + sin_im, cos_im - sin_re
        edge_re = spec[512 + c : 513 + c, :KEPT] - spec[516 + c : 517 + c, KEPT:]
        edge_im = -spec[516 + c : 517 + c, :KEPT] - spec[512 + c : 513 + c, KEPT:]
        down_re = jnp.where(top, edge_re, cos_re - sin_im)
        down_im = jnp.where(top, edge_im, -cos_im - sin_re)
        filt_re, filt_im = filt_p[0, c, 0:64], filt_p[1, c, 0:64]
        up_re, up_im = filt_re * up_re - filt_im * up_im, filt_re * up_im + filt_im * up_re
        filt_re, filt_im = filt_p[0, c, 64:128], filt_p[1, c, 64:128]
        down_re, down_im = filt_re * down_re - filt_im * down_im, filt_re * down_im + filt_im * down_re
        ends_re.append(jnp.concatenate([down_re[0:1], -down_im[0:1]], axis=1))
        ends_im.append(jnp.concatenate([-down_im[0:1], -down_re[0:1]], axis=1))
        down_re, down_im = jnp.where(top, 0.0, down_re), jnp.where(top, 0.0, down_im)
        both = jnp.concatenate(
            [
                jnp.concatenate([up_re + down_re, -(up_im + down_im)], axis=1),
                jnp.concatenate([up_im - down_im, up_re - down_re], axis=1),
            ],
            axis=0,
        )
        store3(resp, pl.ds(at, 128), 0, 2 * KEPT, 2 * KEPT, both)
    both = jnp.concatenate(ends_re + ends_im + [jnp.zeros((8, 2 * KEPT), F32)], axis=0)
    store3(resp, pl.ds(512, 16), 0, 2 * KEPT, 2 * KEPT, both)

    wave[...] = dot(resp[...], tab[...])
    edge = wave[512:516, :] * edge_v[0:1, :] - wave[516:520, :] * edge_v[1:2, :]
    ends[0:4, :] = edge

    for c in range(WIDTH):
        top = lax.broadcasted_iota(jnp.int32, (PAIRS, TOKENS), 0) == 0
        start = c * 128
        for p in range(2):
            at = pl.ds(p * TOKENS, TOKENS)
            re, im = wave[pl.ds(start, 64), at], wave[pl.ds(start + 64, 64), at]
            cos, sin = twist_v[0, :, at], twist_v[1, :, at]
            low = jnp.where(top, ends[pl.ds(c, 1), at], im * cos + re * sin)
            both = jnp.concatenate([re * cos - im * sin, low], axis=0)
            high, low = halves(both)
            for i, part in enumerate([high, high, low]):
                back[c, i * 256 + p * 128 : i * 256 + p * 128 + 128, :] = part
        result = dot(last_v[...], back[c])
        conv[c] = (result * (1.0 / SEQ) + skip[c] * z[c].astype(F32)).astype(BF16)


def kernel(
    tokens, gate, filt, skip, kept, weight, blocks, twist, edge, first, last, pack, moves, mirror,
    out,
    tok_v, filt_v, blocks_v, twist_v, edge_v, first_v, last_v, pack_v, moves_v, mirror_v,
    sent, got, z, tab, turned, filt_p, ends, turn, spec, resp, wave, back, conv, packed, returned, near, near_gate, near_out,
    gate_v, gated_near, gated_far, side, total, w_v,
    local, own, a_send, a_recv, g_send, g_recv, w_send, w_recv, b_send, b_recv, n_send, n_recv, m_send, m_recv,
):
    row, col = lax.axis_index("row"), lax.axis_index("col")
    zh, x, core = row // 8, lax.rem(row, 8) // 2, lax.rem(row, 2)
    low_row = lax.rem(row, 8)
    zl, y = col // 4, lax.rem(col, 4)
    as_tokens, as_channels = row * 16 + col, col * 16 + row

    same = pl.multiple_of(zh * 32, 32)
    cross = pl.multiple_of(32 - zh * 32, 32)
    loads = [
        pltpu.make_async_copy(src, dst, local.at[i])
        for i, (src, dst) in enumerate(
            [(tokens, tok_v), (pack, pack_v), (blocks, blocks_v), (moves, moves_v), (first, first_v),
             (twist, twist_v), (last, last_v), (edge, edge_v), (mirror, mirror_v),
             (gate.at[pl.ds(same, 32), :], near_gate)]
            + [(filt.at[i, :, c, :], filt_v.at[i, c]) for i in range(2) for c in range(WIDTH)]
        )
    ]
    for load in loads[:2]:
        load.start()

    barrier = pltpu.get_barrier_semaphore()

    columns_on = [lax.rem(col + i, 16) for i in range(16)]

    def greet(to_row, steps):
        for i in steps:
            pl.semaphore_signal(barrier, inc=1, device_id=(to_row, columns_on[i]), device_id_type=MESH)

    greet(row, range(1, 16))

    @pl.loop(1, 16)
    def _(s):
        greet(lax.rem(row + s, 16), range(16))

    def columns(part, width):
        return pl.ds(pl.multiple_of(core * 1024 + part * 128, 128), width)

    slices = [columns(x, 128), columns(4 + x, 128)]
    own_weight = [
        pltpu.make_async_copy(weight.at[:, at], w_v.at[zl, y, :, at], own.at[i]) for i, at in enumerate(slices)
    ]
    for load in own_weight:
        load.start()

    loads[0].wait()
    loads[1].wait()

    @pl.loop(0, 2)
    def _(part):
        wide = []
        for i in range(4):
            at = pl.ds(pl.multiple_of((part * 4 + i) * 128, 128), 128)
            wide.append(jnp.concatenate([tok_v[pl.ds(h * 128, 128), at] for h in range(CHUNKS)], axis=1))
        rows = [dot_nt(pack_v[...], jnp.concatenate(wide[i : i + 2], axis=0)).astype(BF16) for i in (0, 2)]
        for i in range(4):
            at = pl.ds(pl.multiple_of((part * 4 + i) * 512, 512), 512)
            sent[at, :] = rows[i // 2][:, i % 2 * 128 : i % 2 * 128 + 128]

    pl.semaphore_wait(barrier, DEVICES - 1)

    def tile(index):
        return pl.ds(pl.multiple_of(index * TILE, TILE), TILE)

    def weight_copy(stage, src, dst, device):
        return pltpu.make_async_remote_copy(
            src_ref=src, dst_ref=dst, send_sem=w_send.at[stage], recv_sem=w_recv.at[stage],
            device_id=device, device_id_type=MESH,
        )

    for s in range(1, 4):
        for at in slices:
            weight_copy(0, weight.at[:, at], w_v.at[zl, y, :, at], (row, lax.rem(zl + s, 4) * 4 + y)).start()

    own_tile = pltpu.make_async_copy(sent.at[tile(as_channels)], got.at[tile(as_tokens)], a_recv)
    own_tile.start()

    def send_tokens(to_row, steps):
        for i in steps:
            pltpu.make_async_remote_copy(
                src_ref=sent.at[tile(columns_on[i] * 16 + to_row)], dst_ref=got.at[tile(as_tokens)],
                send_sem=a_send, recv_sem=a_recv, device_id=(to_row, columns_on[i]), device_id_type=MESH,
            ).start()

    send_tokens(row, range(1, 16))

    @pl.loop(1, 16)
    def _(s):
        send_tokens(lax.rem(row + s, 16), range(16))

    for load in loads[2:]:
        load.start()
    def at_x(other):
        return (zh * 8 + lax.rem(other + 4, 4) * 2 + core, col)

    def at_y(other):
        return (row, zl * 4 + lax.rem(other + 4, 4))

    for load in loads[2:]:
        load.wait()
    prepare(kept, blocks_v, filt_v, mirror_v, tab, turned, filt_p)

    def weight_wait(sem, stage, ref):
        pltpu.make_async_copy(ref, ref, sem.at[stage]).wait()

    for load in own_weight:
        load.wait()
    weight_wait(w_recv, 0, w_v.at[0, pl.ds(0, 3), :, pl.ds(0, 256)])
    for s in range(1, 4):
        part = w_v.at[:, y, :, slices[0]]
        weight_copy(1, part, part, at_y(y + s)).start()
        part = w_v.at[:, y, :, slices[1]]
        weight_copy(1, part, part, at_x(x + s)).start()

    pltpu.make_async_copy(got, got, a_recv).wait()

    def far_column(s):
        ahead = lax.rem(col + s - 1 + s // 9, 8)
        return lax.rem(col // 8 + 1 + s // 9, 2) * 8 + ahead

    def gate_at(to_col):
        return gate.at[pl.ds(cross, 32), pl.ds(pl.multiple_of(to_col * TOKENS, TOKENS), TOKENS)]

    own_gate = pltpu.make_async_copy(gate_at(col), gate_v.at[col], g_recv)
    own_gate.start()

    @pl.loop(1, 16)
    def _(s):
        to_col = far_column(s)
        pltpu.make_async_remote_copy(
            src_ref=gate_at(to_col), dst_ref=gate_v.at[col], send_sem=g_send, recv_sem=g_recv,
            device_id=(row, to_col), device_id_type=MESH,
        ).start()

    weight_wait(w_recv, 1, w_v.at[:, pl.ds(0, 3), :, pl.ds(0, 256)])
    for step in (1, -1):
        part = w_v.at[:, :, :, slices[0]]
        weight_copy(2, part, part, at_x(x + step)).start()
        part = w_v.at[:, y, :, columns(4, 512)]
        weight_copy(2, part, part, at_y(y + step)).start()

    def group(ref, g):
        return ref[pl.ds(pl.multiple_of(g * 256, 256), 256), :]

    def moved(which, pieces):
        rows = [dot(moves_v[which], jnp.concatenate(pieces[i : i + 2], axis=1)) for i in range(0, len(pieces), 2)]
        return [half for pair in rows for half in (pair[:, :128], pair[:, 128:])]

    @pl.loop(0, 4)
    def _(part):
        rows = moved(0, [group(got, part * 4 + i) for i in range(4)])
        for i in range(4):
            piece = rows[i].astype(BF16)
            for c in range(WIDTH):
                for h in range(CHUNKS):
                    at = (c * 4 + h) * 16
                    z[c, tile(part * 4 + i), pl.ds(h * 128, 128)] = piece[at : at + 16, :]

    convolve(z, first_v, last_v, twist_v, edge_v, tab, turned, filt_p, skip, ends, turn, spec, resp, wave, back, conv)

    def pack_rows(part):
        pieces = []
        for i in range(4):
            at = tile(part * 4 + i)
            rows = [conv[c, at, pl.ds(h * 128, 128)] for c in range(WIDTH) for h in range(CHUNKS)]
            pieces.append(jnp.concatenate(rows, axis=0))
        rows = moved(1, pieces)
        for i in range(4):
            packed[pl.ds(pl.multiple_of((part * 4 + i) * 256, 256), 256), :] = rows[i].astype(BF16)

    pl.loop(0, 2)(pack_rows)

    def row_tiles(index):
        return pl.ds(pl.multiple_of(index * 256, 256), 256)

    def send_near():
        @pl.loop(1, 8)
        def _(s):
            to_row = zh * 8 + lax.rem(low_row + s, 8)
            pltpu.make_async_remote_copy(
                src_ref=packed.at[row_tiles(to_row)], dst_ref=near.at[row_tiles(low_row)],
                send_sem=n_send, recv_sem=n_recv, device_id=(to_row, col), device_id_type=MESH,
            ).start()

    def send_far(s):
        to_row = (1 - zh) * 8 + lax.rem(low_row + s, 8)
        for to_col in columns_on:
            pltpu.make_async_remote_copy(
                src_ref=packed.at[tile(to_row * 16 + to_col)], dst_ref=returned.at[tile(col * 8 + low_row)],
                send_sem=b_send, recv_sem=b_recv, device_id=(to_row, to_col), device_id_type=MESH,
            ).start()

    pl.when(zh == 0)(send_near)

    @pl.when(zh == 1)
    def _():
        pl.loop(0, 3)(send_far)

    pl.loop(2, 4)(pack_rows)

    own_near = pltpu.make_async_copy(packed.at[row_tiles(row)], near.at[row_tiles(low_row)], n_recv)
    own_near.start()

    @pl.when(zh == 0)
    def _():
        pl.loop(0, 3)(send_far)

    pl.when(zh == 1)(send_near)

    pl.loop(3, 8)(send_far)

    weight_wait(w_recv, 2, w_v.at[:, :, :, pl.ds(0, 512)])
    for step, rows in ((1, pl.ds(0, 2)), (-1, pl.ds(2, 2))):
        part = w_v.at[rows, :, :, columns(lax.rem(x - step + 4, 4), 128)]
        weight_copy(3, part, part, at_x(x + step)).start()
        part = w_v.at[rows, lax.rem(y - step + 4, 4), :, columns(4, 512)]
        weight_copy(3, part, part, at_y(y + step)).start()

    pltpu.make_async_copy(near, near, n_recv).wait()

    @pl.loop(0, 2)
    def _(part):
        pieces = []
        for n in range(4):
            at = part * 8 + n * 2
            rows = [near[tile(s * 16 + at + i), :] for i in range(2) for s in range(8)]
            pieces.append(jnp.concatenate(rows, axis=0))
        rows = moved(2, pieces)
        for n in range(8):
            for h in range(CHUNKS):
                at = pl.ds(pl.multiple_of((part * 8 + n) * TOKENS + h * 128, 128), 128)
                from_row = n % 2 * 128 + h * 32
                piece = rows[n // 2][from_row : from_row + 32] * near_gate[:, at].astype(F32)
                near_out[part * 8 + n, :, pl.ds(h * 128, 128)] = piece.astype(BF16)

    mine = gated_near.at[col]
    own_out = pltpu.make_async_copy(near_out.at[col], mine, m_recv)
    own_out.start()

    @pl.loop(1, 16)
    def _(s):
        to_col = far_column(s)
        pltpu.make_async_remote_copy(
            src_ref=near_out.at[to_col], dst_ref=mine, send_sem=m_send, recv_sem=m_recv,
            device_id=(row, to_col), device_id_type=MESH,
        ).start()

    weight_wait(w_recv, 3, w_v.at[:, :, :, pl.ds(0, 256)])
    half = w_v.at[:, :, :, columns(0, 1024)]
    weight_copy(4, half, half, (row + 1 - 2 * core, col)).start()

    pltpu.make_async_copy(gate_v, gate_v, g_recv).wait()
    pltpu.make_async_copy(returned, returned, b_recv).wait()

    @pl.loop(0, 2)
    def _(part):
        rows = moved(2, [group(returned, part * 4 + i) for i in range(4)])
        for n in range(8):
            for h in range(CHUNKS):
                at = pl.ds(h * 128, 128)
                from_row = n % 2 * 128 + h * 32
                piece = rows[n // 2][from_row : from_row + 32] * gate_v[part * 8 + n, :, at].astype(F32)
                gated_far[part * 8 + n, :, at] = piece.astype(BF16)

    weight_wait(w_recv, 4, w_v.at[:, :, :, pl.ds(0, 1024)])

    def project(start, at):
        return dot(side[...], w_v[:, :, pl.ds(start, 32), at].reshape(512, 512))

    side[...] = gated_far[...].reshape(512, TOKENS).T

    @pl.loop(0, 4)
    def _(n):
        at = pl.ds(pl.multiple_of(n * 512, 512), 512)
        total[:, at] = project(cross, at)

    pltpu.make_async_copy(near_out, near_out, m_recv).wait()
    side[...] = gated_near[...].reshape(512, TOKENS).T

    @pl.loop(0, 4)
    def _(n):
        at = pl.ds(pl.multiple_of(n * 512, 512), 512)
        out[:, at] = (total[:, at] + project(same, at)).astype(BF16)

    pltpu.make_async_copy(sent.at[pl.ds(0, 4080)], sent.at[pl.ds(0, 4080)], a_send).wait()
    pltpu.make_async_copy(returned, returned, b_send).wait()
    pltpu.make_async_copy(gate_v.at[pl.ds(0, 15)], gate_v.at[pl.ds(0, 15)], g_send).wait()
    pltpu.make_async_copy(near.at[pl.ds(0, 1792)], near.at[pl.ds(0, 1792)], n_send).wait()
    pltpu.make_async_copy(near_out.at[pl.ds(0, 15)], near_out.at[pl.ds(0, 15)], m_send).wait()
    weight_wait(w_send, 0, w_v.at[0, pl.ds(0, 3), :, pl.ds(0, 256)])
    weight_wait(w_send, 1, w_v.at[:, pl.ds(0, 3), :, pl.ds(0, 256)])
    weight_wait(w_send, 2, w_v.at[:, :, :, pl.ds(0, 512)])
    weight_wait(w_send, 3, w_v.at[:, :, :, pl.ds(0, 256)])
    weight_wait(w_send, 4, w_v.at[:, :, :, pl.ds(0, 1024)])


def on_device(tokens, gate, filter_spectrum, skip_gain, kept_blocks, out_weight):
    constants = [jnp.asarray(t) for t in tables()]
    filt = jnp.transpose(filter_spectrum, (0, 1, 3, 2))
    hbm = pl.BlockSpec(memory_space=pl.ANY)
    vmem = pl.BlockSpec(memory_space=pltpu.VMEM)
    smem = pl.BlockSpec(memory_space=pltpu.SMEM)
    like = lambda t: pltpu.VMEM(t.shape, t.dtype)
    dma = pltpu.SemaphoreType.DMA
    blocks, twist, edge, first, last, pack, moves, mirror = constants
    return pl.pallas_call(
        kernel,
        out_shape=pltpu.VMEM((TOKENS, FEATS), BF16),
        in_specs=[hbm, hbm, hbm, smem, vmem, hbm] + [hbm] * 8,
        out_specs=vmem,
        scratch_shapes=[
            like(tokens), pltpu.VMEM((2, WIDTH, KEPT, BLOCK), F32), like(blocks), like(twist), like(edge), like(first), like(last), like(pack),
            like(moves), like(mirror),
            pltpu.VMEM((4096, 128), BF16),
            pltpu.VMEM((4096, 128), BF16),
            pltpu.VMEM((WIDTH, 256, TOKENS), BF16),
            pltpu.VMEM((6 * KEPT, BLOCKS), BF16),
            pltpu.VMEM((3 * BLOCKS, 2 * KEPT), BF16),
            pltpu.VMEM((2, WIDTH, BLOCK, KEPT), F32),
            pltpu.VMEM((8, BLOCKS), F32),
            pltpu.VMEM((528, 3 * BLOCKS), BF16),
            pltpu.VMEM((528, 2 * KEPT), F32),
            pltpu.VMEM((528, 6 * KEPT), BF16),
            pltpu.VMEM((528, BLOCKS), F32),
            pltpu.VMEM((WIDTH, 768, TOKENS), BF16),
            pltpu.VMEM((WIDTH, 256, TOKENS), BF16),
            pltpu.VMEM((4096, 128), BF16),
            pltpu.VMEM((2048, 128), BF16),
            pltpu.VMEM((2048, 128), BF16),
            pltpu.VMEM((32, 16 * TOKENS), BF16),
            pltpu.VMEM((16, 32, TOKENS), BF16),
            pltpu.VMEM((16, 32, TOKENS), BF16),
            pltpu.VMEM((16, 32, TOKENS), BF16),
            pltpu.VMEM((16, 32, TOKENS), BF16),
            pltpu.VMEM((TOKENS, 512), BF16),
            pltpu.VMEM((TOKENS, FEATS), F32),
            pltpu.VMEM((4, 4, 64, FEATS), BF16),
            dma((18,)), dma((2,)), dma, dma, dma, dma, dma((5,)), dma((5,)), dma, dma, dma, dma, dma, dma,
        ],
        compiler_params=pltpu.CompilerParams(
            collective_id=0, has_side_effects=True, vmem_limit_bytes=56 * 1024 * 1024
        ),
    )(tokens, gate.T, filt, skip_gain, kept_blocks.reshape(1, KEPT), out_weight, *constants)


def solution(mesh):
    return jax.shard_map(
        on_device,
        mesh=mesh,
        in_specs=(
            P(("row", "col"), None),
            P("row", "col"),
            P(None, None, None, ("col", "row")),
            P(("col", "row")),
            P(),
            P("col", None),
        ),
        out_specs=P(("row", "col"), None),
        check_vma=False,
    )
```
